32 devices in a mesh: seq: 16 (over z, y, x), rep: 2 (over core).
Axes of the slice: x: 2, y: 2, z: 4, core: 2. Of those that a mesh axis runs over, the one named last changes fastest.
Arguments:
- block_in: bfloat16 [2, 2048, 2048], P('rep', 'seq'), may hold values from -6 to 6
- cotangent: bfloat16 [2, 2048, 2048], P('rep', 'seq'), may hold values from -6 to 6
- domain_ids: int32 [2], replicated, may hold values from 0 to 2
- domain_weight: float32 [3], replicated, may hold values from 0.5 to 2
- lower_bound: float32 [2048], P('seq'), may hold values from 0 to 0.9998
- in_w: float32 [2048, 6144], P(('seq', 'rep')), may hold values from -0.125 to 0.125
- out_w: float32 [2048, 2048], P(('seq', 'rep')), may hold values from -0.125 to 0.125
- glu_w: float32 [2048, 11264], P(('seq', 'rep')), may hold values from -0.125 to 0.125
- down_w: float32 [5632, 2048], P(('seq', 'rep')), may hold values from -0.078125 to 0.078125
- gains: float32 [3, 2048], P(None, ('seq', 'rep')), may hold values from 0.8 to 6
- in_m: float32 [2048, 6144], P(('seq', 'rep')), may hold values from -9.1552734e-05 to 9.1552734e-05
- out_m: float32 [2048, 2048], P(('seq', 'rep')), may hold values from -9.1552734e-05 to 9.1552734e-05
- glu_m: float32 [2048, 11264], P(('seq', 'rep')), may hold values from -9.1552734e-05 to 9.1552734e-05
- down_m: float32 [5632, 2048], P(('seq', 'rep')), may hold values from -9.1552734e-05 to 9.1552734e-05
- gain_m: float32 [3, 2048], P(None, ('seq', 'rep')), may hold values from -9.1552734e-05 to 9.1552734e-05
- in_v: float32 [2048, 6144], P(('seq', 'rep')), may hold values from 5.8381244e-10 to 7.784165e-09
- out_v: float32 [2048, 2048], P(('seq', 'rep')), may hold values from 5.8381244e-10 to 7.784165e-09
- glu_v: float32 [2048, 11264], P(('seq', 'rep')), may hold values from 5.8381244e-10 to 7.784165e-09
- down_v: float32 [5632, 2048], P(('seq', 'rep')), may hold values from 5.8381244e-10 to 7.784165e-09
- gain_v: float32 [3, 2048], P(None, ('seq', 'rep')), may hold values from 5.8381244e-10 to 7.784165e-09
Outputs:
- block_out: bfloat16 [2, 2048, 2048], P('rep', 'seq')
- grad_block: float32 [2, 2048, 2048], P('rep', 'seq')
- in_new: float32 [2048, 6144], P(('seq', 'rep'))
- out_new: float32 [2048, 2048], P(('seq', 'rep'))
- glu_new: float32 [2048, 11264], P(('seq', 'rep'))
- down_new: float32 [5632, 2048], P(('seq', 'rep'))
- gain_new: float32 [3, 2048], P(None, ('seq', 'rep'))
- in_m_new: float32 [2048, 6144], P(('seq', 'rep'))
- out_m_new: float32 [2048, 2048], P(('seq', 'rep'))
- glu_m_new: float32 [2048, 11264], P(('seq', 'rep'))
- down_m_new: float32 [5632, 2048], P(('seq', 'rep'))
- gain_m_new: float32 [3, 2048], P(None, ('seq', 'rep'))
- in_v_new: float32 [2048, 6144], P(('seq', 'rep'))
- out_v_new: float32 [2048, 2048], P(('seq', 'rep'))
- glu_v_new: float32 [2048, 11264], P(('seq', 'rep'))
- down_v_new: float32 [5632, 2048], P(('seq', 'rep'))
- gain_v_new: float32 [3, 2048], P(None, ('seq', 'rep'))
- grad_norm: float32 [], replicated
The draws below stay inside these ranges and needn't reach their ends.
All inputs are finite; a program needn't handle non-finite values.
Results may differ from the reference program's by a relative error of at most 0.012.
The reference program's roundings to bfloat16 on the way count: a program that leaves them out, or rounds other values in their place, can miss the bound.
Values may be sent and summed in bfloat16 or wider, within the bound.
No kernel may reach another device: no remote copies, remote signals or barrier semaphores. Data moves between devices by JAX's collectives and lax.ppermute only.
A program may use at most 344 MiB of HBM per device.

```python
import math
import jax
import jax.numpy as jnp
from jax import lax

D = 2048
FF = 5632
DOMS = 3
STEP = 10
GTOK = 2048
SEQS = 2
N_REP = 2


def draw_lower_bound(key, part):
    key = jax.random.fold_in(key, 11)
    power = jax.random.uniform(key, (D,), jnp.float32, -3.3, -0.3)
    return 1.0 - jnp.power(10.0, power)


def draw_gains(key, part):
    key = jax.random.fold_in(key, 23)
    place = jnp.arange(D, dtype=jnp.float32) / (D - 1)
    rising = 2.0
    jitter = jax.random.uniform(key, (3, D), jnp.float32, -0.15, 0.15)
    return (1.0 + rising * place)[None, :] * (1.0 + jitter)


def block_levels(rng, dims, cuts, low, top_value):
    def one(dim, blocks):
        steps = jax.random.uniform(jax.random.fold_in(jax.random.fold_in(rng, 6), dim), (blocks,), jnp.float32, low / len(cuts), top_value / len(cuts))
        return jnp.repeat(jnp.exp(steps), dims[dim] // blocks).reshape((-1,) + (1,) * (len(dims) - dim - 1))

    gain = one(*cuts[0])
    for cut in cuts[1:]:
        gain = gain * one(*cut)
    return gain


def noise(key, shape, spread, bound, split=(), held_as=jnp.bfloat16):
    drawn = spread * jax.random.normal(key, shape, jnp.float32)
    if split:
        drawn = drawn * block_levels(key, shape, split, -0.22, 0.18)
    return jnp.clip(drawn, -bound, bound).astype(held_as)


def setup_inputs(seed: int = 0) -> dict:
    key_list = jax.random.split(jax.random.key(seed), 21)
    block_in = noise(key_list[0], (N_REP, GTOK, D), 1.0, 6.0, ((0, 2), (1, 16)))
    cotangent = noise(key_list[1], (N_REP, GTOK, D), 1.0, 6.0, ((0, 2), (1, 16)))
    domain_ids = jax.random.randint(key_list[2], (SEQS,), 0, DOMS).astype(jnp.int32)
    domain_weight = jnp.clip(jax.random.uniform(key_list[3], (DOMS,), jnp.float32, 0.5, 2.0), 0.5, 2.0)
    lower_bound = draw_lower_bound(jax.random.fold_in(key_list[20], 71), 0)
    in_w = noise(key_list[5], (D, 3 * D), D ** -0.5, 0.125, ((0, 32),), jnp.float32)
    out_w = noise(key_list[6], (D, D), D ** -0.5, 0.125, ((0, 32),), jnp.float32)
    glu_w = noise(key_list[7], (D, 2 * FF), D ** -0.5, 0.125, ((0, 32),), jnp.float32)
    down_w = noise(key_list[8], (FF, D), FF ** -0.5, 0.078125, ((0, 32),), jnp.float32)
    gains = draw_gains(jax.random.fold_in(key_list[20], 71), 0)
    in_m = noise(key_list[10], (D, 3 * D), (0.11 / (4 * D * D + 3 * D * FF + 3 * D) ** 0.5), 9.1552734375e-05, ((0, 32),), jnp.float32)
    out_m = noise(key_list[11], (D, D), (0.11 / (4 * D * D + 3 * D * FF + 3 * D) ** 0.5), 9.1552734375e-05, ((0, 32),), jnp.float32)
    glu_m = noise(key_list[12], (D, 2 * FF), (0.11 / (4 * D * D + 3 * D * FF + 3 * D) ** 0.5), 9.1552734375e-05, ((0, 32),), jnp.float32)
    down_m = noise(key_list[13], (FF, D), (0.11 / (4 * D * D + 3 * D * FF + 3 * D) ** 0.5), 9.1552734375e-05, ((0, 32),), jnp.float32)
    gain_m = noise(key_list[14], (3, D), (0.11 / (4 * D * D + 3 * D * FF + 3 * D) ** 0.5), 9.1552734375e-05, ((1, 32),), jnp.float32)
    in_v = jnp.clip(jnp.exp(math.log(7.78416531233006e-09) - 2.5902671 * jax.random.uniform(key_list[15], (D, 3 * D), jnp.float32) ** block_levels(key_list[15], (D, 3 * D), ((0, 32),), -0.2, 0.2)), 5.838124428336755e-10, 7.78416531233006e-09)
    out_v = jnp.clip(jnp.exp(math.log(7.78416531233006e-09) - 2.5902671 * jax.random.uniform(key_list[16], (D, D), jnp.float32) ** block_levels(key_list[16], (D, D), ((0, 32),), -0.2, 0.2)), 5.838124428336755e-10, 7.78416531233006e-09)
    glu_v = jnp.clip(jnp.exp(math.log(7.78416531233006e-09) - 2.5902671 * jax.random.uniform(key_list[17], (D, 2 * FF), jnp.float32) ** block_levels(key_list[17], (D, 2 * FF), ((0, 32),), -0.2, 0.2)), 5.838124428336755e-10, 7.78416531233006e-09)
    down_v = jnp.clip(jnp.exp(math.log(7.78416531233006e-09) - 2.5902671 * jax.random.uniform(key_list[18], (FF, D), jnp.float32) ** block_levels(key_list[18], (FF, D), ((0, 32),), -0.2, 0.2)), 5.838124428336755e-10, 7.78416531233006e-09)
    gain_v = jnp.clip(jnp.exp(math.log(7.78416531233006e-09) - 2.5902671 * jax.random.uniform(key_list[19], (3, D), jnp.float32) ** block_levels(key_list[19], (3, D), ((1, 32),), -0.2, 0.2)), 5.838124428336755e-10, 7.78416531233006e-09)
    return dict(block_in=block_in, cotangent=cotangent, domain_ids=domain_ids, domain_weight=domain_weight, lower_bound=lower_bound, in_w=in_w, out_w=out_w, glu_w=glu_w, down_w=down_w, gains=gains, in_m=in_m, out_m=out_m, glu_m=glu_m, down_m=down_m, gain_m=gain_m, in_v=in_v, out_v=out_v, glu_v=glu_v, down_v=down_v, gain_v=gain_v)


NORM_EPS = 1e-06
CLIP_LIMIT = 1.0
BETA_FIRST = 0.9
BETA_SECOND = 0.95
ADAM_EPS = 1e-08
MATRIX_RATE = 0.04
GAIN_RATE = 0.4
MATRIX_DECAY = 0.1

@jax.custom_vjp
def low(v):
    return lax.optimization_barrier(v.astype(jnp.bfloat16)).astype(jnp.float32)

@jax.custom_vjp
def low_back(v):
    return v

def low_keep(v):
    return (low(v), None)

def low_pass(kept, grad):
    return (grad,)

def back_keep(v):
    return (v, None)

def back_low(kept, grad):
    return (low(grad),)
low.defvjp(low_keep, low_pass)
low_back.defvjp(back_keep, back_low)

def combine_steps(earlier, later):
    return (earlier[0] * later[0], later[0] * earlier[1] + later[1])

def inverse_rms(values):
    return lax.rsqrt(lax.optimization_barrier(jnp.mean(values * values, axis=-1, keepdims=True)) + NORM_EPS)

def product(left_side, right_side):
    return jnp.dot(left_side, right_side, precision=lax.Precision.HIGHEST, preferred_element_type=jnp.float32)

def sequence_weights(domain_ids, domain_weight):
    kinds = domain_weight.shape[0]
    total = domain_ids.shape[0]
    same_kind = (domain_ids[:, None] == domain_ids[None, :]).astype(jnp.float32)
    counts = lax.optimization_barrier(jnp.sum(same_kind, axis=1))
    onehot = (domain_ids[:, None] == jnp.arange(kinds, dtype=jnp.int32)[None, :]).astype(jnp.float32)
    chosen = lax.optimization_barrier(jnp.sum(onehot * domain_weight[None, :], axis=1))
    return chosen * (total / kinds) / counts

def forward(params, tokens_f, lower_bound):
    in_w, out_w, glu_w, down_w, gains = params
    width = tokens_f.shape[1]
    hidden_width = down_w.shape[0]
    in_b = low(in_w)
    out_b = low(out_w)
    glu_b = low(glu_w)
    down_b = low(down_w)
    gain_b = low(gains)
    normed = low(tokens_f * inverse_rms(tokens_f) * gain_b[0])
    proj = low_back(product(normed, in_b))
    in_raw = low(proj[:, :width])
    forget_raw = low(proj[:, width:2 * width])
    gate_raw = proj[:, 2 * width:]
    forget = lower_bound + (1.0 - lower_bound) * jax.nn.sigmoid(forget_raw)
    drive = jax.nn.silu(in_raw) * (1.0 - forget)
    _, state = lax.associative_scan(combine_steps, (forget, drive), axis=0)
    state = low_back(low(state))
    gated = low(state * inverse_rms(state) * gain_b[1] * jax.nn.silu(gate_raw))
    resid = tokens_f + low_back(product(gated, out_b))
    second = low(resid * inverse_rms(resid) * gain_b[2])
    paired = low_back(product(second, glu_b))
    hidden = low(jax.nn.silu(paired[:, :hidden_width]) * paired[:, hidden_width:])
    return resid + low_back(product(hidden, down_b))

def adam_step(weight, first, second_m, grad, factor, rate, decay):
    clipped = grad * factor
    first_new = BETA_FIRST * first + (1.0 - BETA_FIRST) * clipped
    second_new = BETA_SECOND * second_m + (1.0 - BETA_SECOND) * clipped * clipped
    first_hat = first_new / (1.0 - BETA_FIRST ** STEP)
    second_hat = second_new / (1.0 - BETA_SECOND ** STEP)
    weight_new = weight - rate * (first_hat / (jnp.sqrt(second_hat) + ADAM_EPS) + decay * weight)
    return (first_new, second_new, weight_new)

def add_trees(first_tree, second_tree):
    return jax.tree.map(jnp.add, first_tree, second_tree)

def reference(block_in, cotangent, domain_ids, domain_weight, lower_bound, in_w, out_w, glu_w, down_w, gains, in_m, out_m, glu_m, down_m, gain_m, in_v, out_v, glu_v, down_v, gain_v):
    groups, group_tokens, width = block_in.shape
    seq_total = domain_ids.shape[0]
    length = groups * group_tokens // seq_total
    seq_scale = sequence_weights(domain_ids, domain_weight)
    params = (in_w, out_w, glu_w, down_w, gains)
    inputs_all = block_in.astype(jnp.float32).reshape(seq_total, length, width)
    grads_all = cotangent.astype(jnp.float32).reshape(seq_total, length, width) * seq_scale[:, None, None]

    def one_sequence(totals, pair):
        tokens_f, grad_output = pair
        output, pullback = jax.vjp(lambda weights, values: forward(weights, values, lower_bound), params, tokens_f)
        grad_params, grad_tokens = pullback(grad_output)
        return (add_trees(totals, grad_params), (output.astype(jnp.bfloat16), grad_tokens))
    zeros = jax.tree.map(jnp.zeros_like, params)
    grads, (outputs, grad_inputs) = lax.scan(one_sequence, zeros, (inputs_all, grads_all))
    squares = jnp.float32(0.0)
    for grad in grads:
        squares = squares + jnp.sum(grad * grad)
    grad_norm = jnp.sqrt(squares)
    factor = jnp.minimum(1.0, CLIP_LIMIT / (grad_norm + 1e-06))
    in_res = adam_step(in_w, in_m, in_v, grads[0], factor, MATRIX_RATE, MATRIX_DECAY)
    out_res = adam_step(out_w, out_m, out_v, grads[1], factor, MATRIX_RATE, MATRIX_DECAY)
    glu_res = adam_step(glu_w, glu_m, glu_v, grads[2], factor, MATRIX_RATE, MATRIX_DECAY)
    down_res = adam_step(down_w, down_m, down_v, grads[3], factor, MATRIX_RATE, MATRIX_DECAY)
    gain_res = adam_step(gains, gain_m, gain_v, grads[4], factor, GAIN_RATE, 0.0)
    block_out = outputs.reshape(groups, group_tokens, width)
    grad_block = grad_inputs.reshape(groups, group_tokens, width)
    return (block_out, grad_block, in_res[2], out_res[2], glu_res[2], down_res[2], gain_res[2], in_res[0], out_res[0], glu_res[0], down_res[0], gain_res[0], in_res[1], out_res[1], glu_res[1], down_res[1], gain_res[1], grad_norm)
```

```python
import functools

import jax
import jax.numpy as jnp
import numpy as np
from jax import lax
from jax.experimental import pallas as pl
from jax.experimental.pallas import tpu as pltpu
from jax.sharding import Mesh, PartitionSpec as P

STEP = 10

NORM_EPS = 1e-06
CLIP_LIMIT = 1.0
BETA_FIRST = 0.9
BETA_SECOND = 0.95
ADAM_EPS = 1e-08
MATRIX_RATE = 0.04
GAIN_RATE = 0.4
MATRIX_DECAY = 0.1

LINE = "z"
PLANE = ("y", "x")
CORE = "core"
OWNERS = ("z", "core")


def contract(left_side, right_side, left_dim, right_dim):
    return lax.dot_general(
        left_side,
        right_side,
        (((left_dim,), (right_dim,)), ((), ())),
        preferred_element_type=jnp.float32,
    )


def rounded(values):
    return lax.reduce_precision(values, exponent_bits=8, mantissa_bits=7)


def silu_slope(values):
    logistic = jax.nn.sigmoid(values)
    return logistic * (1.0 + values * (1.0 - logistic))


def sequence_weights(domain_ids, domain_weight):
    kinds = domain_weight.shape[0]
    total = domain_ids.shape[0]
    same_kind = (domain_ids[:, None] == domain_ids[None, :]).astype(jnp.float32)
    counts = jnp.sum(same_kind, axis=1)
    onehot = (domain_ids[:, None] == jnp.arange(kinds, dtype=jnp.int32)[None, :]).astype(
        jnp.float32
    )
    chosen = jnp.sum(onehot * domain_weight[None, :], axis=1)
    return chosen * (total / kinds) / counts


def adam_step(weight, first, second_m, grad, factor, rate, decay):
    clipped = grad * factor
    first_new = BETA_FIRST * first + (1.0 - BETA_FIRST) * clipped
    second_new = BETA_SECOND * second_m + (1.0 - BETA_SECOND) * clipped * clipped
    first_hat = first_new / (1.0 - BETA_FIRST**STEP)
    second_hat = second_new / (1.0 - BETA_SECOND**STEP)
    weight_new = weight - rate * (first_hat / (jnp.sqrt(second_hat) + ADAM_EPS) + decay * weight)
    return (first_new, second_new, weight_new)


def squared(values):
    values = values.astype(jnp.float32)
    return jnp.sum(values * values)


def swap(values, axis, bit):
    size = lax.axis_size(axis)
    return lax.ppermute(values, axis, [(i, i ^ bit) for i in range(size)])


def gather_small(values, axis):
    size = lax.axis_size(axis)
    held = lax.dynamic_update_index_in_dim(
        jnp.zeros((size,) + values.shape, values.dtype), values, lax.axis_index(axis), 0
    )
    bit = 1
    while bit < size:
        held = held + swap(held, axis, bit)
        bit *= 2
    return held


def total_small(values, axes):
    for axis in axes:
        bit = 1
        while bit < lax.axis_size(axis):
            values = values + swap(values, axis, bit)
            bit *= 2
    return values


def gather_plane(values):
    return jnp.concatenate(
        [values] + [swap(values, PLANE, k) for k in range(1, lax.axis_size(PLANE))], axis=0
    )


def total_plane(values):
    size = lax.axis_size(PLANE)
    blocks = values.reshape(size, values.shape[0] // size)
    bit = 1
    while bit < size:
        other = swap(blocks, PLANE, bit)
        blocks = blocks + jnp.stack([other[k ^ bit] for k in range(size)])
        bit *= 2
    return blocks.reshape(values.shape)


def scatter_plane(partial):
    size = lax.axis_size(PLANE)
    rows = partial.shape[0] // size
    total = partial[:rows]
    for k in range(1, size):
        total = total + swap(
            partial[k * rows : (k + 1) * rows].astype(jnp.bfloat16), PLANE, k
        ).astype(jnp.float32)
    return total


def exchange_plane(blocks):
    rank = lax.axis_index(PLANE)
    result = blocks
    for k in range(1, blocks.shape[0]):
        sent = lax.dynamic_index_in_dim(blocks, rank ^ k, 0, keepdims=False)
        result = lax.dynamic_update_index_in_dim(result, swap(sent, PLANE, k), rank ^ k, 0)
    return result


TILE = 8


def gates(proj_ref, rows, width, bound):
    in_raw = proj_ref[rows, 0:width].astype(jnp.bfloat16).astype(jnp.float32)
    forget_raw = proj_ref[rows, width : 2 * width].astype(jnp.bfloat16).astype(jnp.float32)
    forget = bound + (1.0 - bound) * jax.nn.sigmoid(forget_raw)
    return in_raw, forget


def scan_kernel(width, order_ref, proj_ref, bound_ref, state_ref, prod_ref, last_ref):
    blocks = order_ref.shape[0]
    per_block = proj_ref.shape[0] // blocks // TILE
    bound = bound_ref[0:1, :]
    row = lax.broadcasted_iota(jnp.int32, (TILE, width), 0)

    def step(index, carry):
        state_in, prod_in = carry
        tile = order_ref[index // per_block] * per_block + index % per_block
        rows = pl.ds(pl.multiple_of(tile * TILE, TILE), TILE)
        in_raw, forget = gates(proj_ref, rows, width, bound)
        drive = in_raw * jax.nn.sigmoid(in_raw) * (1.0 - forget)
        for shift in (1, 2, 4):
            keep = row >= shift
            drive = jnp.where(keep, forget * pltpu.roll(drive, shift, 0) + drive, drive)
            forget = jnp.where(keep, forget * pltpu.roll(forget, shift, 0), forget)
        state = drive + forget * state_in
        prod = forget * prod_in
        state_ref[rows, :] = state
        prod_ref[rows, :] = prod
        return state[TILE - 1 : TILE, :], prod[TILE - 1 : TILE, :]

    state, prod = lax.fori_loop(
        0,
        blocks * per_block,
        step,
        (jnp.zeros((1, width), jnp.float32), jnp.ones((1, width), jnp.float32)),
    )
    last_ref[0:1, :] = state
    last_ref[1:2, :] = prod


def back_kernel(width, order_ref, proj_ref, bound_ref, grad_ref, carried_ref, prod_ref, last_ref):
    blocks = order_ref.shape[0]
    per_block = proj_ref.shape[0] // blocks // TILE
    count = blocks * per_block
    bound = bound_ref[0:1, :]
    row = lax.broadcasted_iota(jnp.int32, (TILE, width), 0)

    def step(back, carry):
        carried_in, prod_in, forget_next = carry
        index = count - 1 - back
        tile = order_ref[index // per_block] * per_block + index % per_block
        rows = pl.ds(pl.multiple_of(tile * TILE, TILE), TILE)
        _, forget = gates(proj_ref, rows, width, bound)
        rate = jnp.where(row < TILE - 1, pltpu.roll(forget, TILE - 1, 0), forget_next)
        carried = grad_ref[rows, :].astype(jnp.float32)
        for shift in (1, 2, 4):
            keep = row < TILE - shift
            carried = jnp.where(
                keep, rate * pltpu.roll(carried, TILE - shift, 0) + carried, carried
            )
            rate = jnp.where(keep, rate * pltpu.roll(rate, TILE - shift, 0), rate)
        carried = carried + rate * carried_in
        prod = rate * prod_in
        carried_ref[rows, :] = carried
        prod_ref[rows, :] = prod
        return carried[0:1, :], prod[0:1, :], forget[0:1, :]

    ones = jnp.ones((1, width), jnp.float32)
    carried, prod, forget = lax.fori_loop(
        0, count, step, (jnp.zeros((1, width), jnp.float32), ones, ones)
    )
    last_ref[0:1, :] = forget * carried
    last_ref[1:2, :] = forget * prod


def call_scan(kernel, order, *arrays):
    tokens = arrays[0].shape[0]
    width = arrays[1].shape[1]
    vmem = pl.BlockSpec(memory_space=pltpu.VMEM)
    full = jax.ShapeDtypeStruct((tokens, width), jnp.float32)
    return pl.pallas_call(
        functools.partial(kernel, width),
        out_shape=(full, full, jax.ShapeDtypeStruct((2, width), jnp.float32)),
        in_specs=[pl.BlockSpec(memory_space=pltpu.SMEM)] + [vmem] * len(arrays),
        out_specs=(vmem, vmem, vmem),
        compiler_params=pltpu.CompilerParams(vmem_limit_bytes=32 * 1024 * 1024),
    )(order, *arrays)


def on_device(
    block_in,
    cotangent,
    domain_ids,
    domain_weight,
    lower_bound,
    in_w,
    out_w,
    glu_w,
    down_w,
    gains,
    in_m,
    out_m,
    glu_m,
    down_m,
    gain_m,
    in_v,
    out_v,
    glu_v,
    down_v,
    gain_v,
):
    bf16 = jnp.bfloat16
    f32 = jnp.float32
    inputs_f = block_in[0].astype(f32)
    tok, width = inputs_f.shape
    line = lax.axis_size(LINE)
    plane = lax.axis_size(PLANE)
    cores = lax.axis_size(CORE)
    level = lax.axis_index(LINE)
    rank = lax.axis_index(PLANE)
    device = lax.axis_index((LINE,) + PLANE)
    order = jnp.arange(plane, dtype=jnp.int32) ^ rank
    group_seqs = domain_ids.shape[0] // cores
    assert group_seqs == 1
    span = tok * line * plane
    rows = in_w.shape[0]
    chan = lower_bound.shape[0]
    channels = chan * line
    hidden_rows = down_w.shape[0] * cores
    hidden_width = hidden_rows * line

    seq_scale = sequence_weights(domain_ids, domain_weight)
    position = device * tok + jnp.arange(tok, dtype=jnp.int32)
    owner_seq = lax.axis_index(CORE) * group_seqs + position // (span // group_seqs)
    pick = (owner_seq[:, None] == jnp.arange(domain_ids.shape[0], dtype=jnp.int32)[None, :]).astype(
        f32
    )
    row_weight = jnp.sum(pick * seq_scale[None, :], axis=1)

    def feature_swap(values, outer, inner):
        count = values.shape[0]
        return (
            values.reshape(count, line, outer, inner, rows)
            .transpose(0, 1, 3, 2, 4)
            .reshape(count, width)
        )

    in_blocks = (
        in_w.astype(bf16)
        .reshape(rows, 3, line, plane, chan)
        .transpose(3, 0, 1, 2, 4)
        .reshape(plane, rows, 3 * channels)
    )
    in_held = exchange_plane(in_blocks).reshape(plane * rows, 3 * channels)
    in_b = lax.all_gather(in_held, OWNERS, axis=0, tiled=True)
    out_b = lax.all_gather(out_w.astype(bf16), OWNERS, axis=0, tiled=True)
    glu_blocks = (
        glu_w.astype(bf16)
        .reshape(rows, 2, line, plane, hidden_rows)
        .transpose(3, 0, 1, 2, 4)
        .reshape(plane, rows, 2 * hidden_width)
    )
    glu_held = exchange_plane(glu_blocks).reshape(plane * rows, 2 * hidden_width)
    glu_b = lax.all_gather(glu_held, OWNERS, axis=0, tiled=True)
    down_b = lax.all_gather(down_w.astype(bf16), OWNERS, axis=0, tiled=True)

    gain_size = 3 * gains.shape[1]
    packed = jnp.concatenate([rounded(gains).reshape(-1), lower_bound])
    packed = gather_small(packed, LINE)
    bound = packed[:, gain_size:].reshape(1, channels)
    held_gains = gather_small(packed[:, :gain_size], CORE)
    gain_mid = (
        held_gains.reshape(cores, line, 3, gains.shape[1])[:, :, 1]
        .transpose(1, 0, 2)
        .reshape(1, channels)
    )
    held_gains = gather_small(gather_small(held_gains, "x"), "y")
    gain_f = (
        held_gains.reshape(plane, cores, line, 3, gains.shape[1])
        .transpose(3, 2, 0, 1, 4)
        .reshape(3, width)
    )

    grad_output = cotangent[0].astype(f32) * row_weight[:, None]
    grad_output_b = gather_plane(grad_output.astype(bf16))

    scale_one = lax.rsqrt(jnp.mean(inputs_f * inputs_f, axis=1, keepdims=True) + NORM_EPS)
    unit_one = inputs_f * scale_one
    normed = gather_plane(feature_swap((unit_one * gain_f[0]).astype(bf16), plane, cores))
    proj = contract(normed, in_b, 1, 0)
    local_state, local_prod, last = call_scan(scan_kernel, order, proj, bound)
    lasts = gather_small(last, LINE)
    state_in = jnp.zeros((channels,), f32)
    for k in range(line):
        state_in = jnp.where(k < level, lasts[k, 1] * state_in + lasts[k, 0], state_in)
    state = local_state + local_prod * state_in[None, :]
    state_f = rounded(state)
    square_mid = total_plane(jnp.sum(state_f * state_f, axis=1))
    scale_mid = lax.rsqrt(square_mid / width + NORM_EPS)[:, None]
    unit_mid = state_f * scale_mid
    gate_raw = proj[:, 2 * channels :]
    gate_act = jax.nn.silu(gate_raw)
    gated = (unit_mid * gain_mid * gate_act).astype(bf16)
    resid = inputs_f + scatter_plane(contract(gated, out_b, 1, 0))

    scale_two = lax.rsqrt(jnp.mean(resid * resid, axis=1, keepdims=True) + NORM_EPS)
    unit_two = resid * scale_two
    second = gather_plane(feature_swap((unit_two * gain_f[2]).astype(bf16), plane, cores))
    paired = contract(second, glu_b, 1, 0)
    up_gate = paired[:, :hidden_width]
    up_value = paired[:, hidden_width:]
    gate_silu = jax.nn.silu(up_gate)
    hidden = (gate_silu * up_value).astype(bf16)
    output = resid + scatter_plane(contract(hidden, down_b, 1, 0))
    block_out = output.astype(bf16)[None]

    grad_hidden = contract(grad_output_b, down_b, 1, 1)
    grad_paired = jnp.concatenate(
        [grad_hidden * up_value * silu_slope(up_gate), grad_hidden * gate_silu], axis=1
    ).astype(bf16)
    grad_second = feature_swap(scatter_plane(contract(grad_paired, glu_b, 1, 1)), cores, plane)
    glu_part = contract(second, grad_paired, 0, 0).astype(bf16)
    down_part = contract(hidden, grad_output_b, 0, 0).astype(bf16)
    glu_held = lax.psum_scatter(glu_part, OWNERS, scatter_dimension=0, tiled=True)
    down_grad = lax.psum_scatter(down_part, OWNERS, scatter_dimension=0, tiled=True)
    grad_gain_two = jnp.sum(grad_second * unit_two, axis=0)
    weighted_two = grad_second * gain_f[2]
    grad_resid = grad_output + scale_two * (
        weighted_two - unit_two * jnp.mean(weighted_two * unit_two, axis=1, keepdims=True)
    )

    grad_resid_b = gather_plane(grad_resid.astype(bf16))
    grad_gated = contract(grad_resid_b, out_b, 1, 1)
    out_part = contract(gated, grad_resid_b, 0, 0).astype(bf16)
    out_grad = lax.psum_scatter(out_part, OWNERS, scatter_dimension=0, tiled=True)
    grad_gain_mid = jnp.sum(grad_gated * unit_mid * gate_act, axis=0)
    grad_gate = grad_gated * unit_mid * gain_mid * silu_slope(gate_raw)
    weighted_mid = grad_gated * gain_mid * gate_act
    mean_mid = total_plane(jnp.sum(weighted_mid * unit_mid, axis=1)) / width
    grad_state = scale_mid * (weighted_mid - unit_mid * mean_mid[:, None])
    local_carried, local_rate, first = call_scan(
        back_kernel, order, proj, bound, rounded(grad_state)
    )
    firsts = gather_small(first, LINE)
    carried_in = jnp.zeros((channels,), f32)
    for k in range(line - 1, -1, -1):
        carried_in = jnp.where(k > level, firsts[k, 1] * carried_in + firsts[k, 0], carried_in)
    carried = local_carried + local_rate * carried_in[None, :]
    blocked = state.reshape(plane, tok, channels)
    tails = lax.dynamic_update_index_in_dim(
        jnp.zeros((plane, channels), f32), state_in, order[0], 0
    )
    for k in range(1, plane):
        tails = lax.dynamic_update_index_in_dim(
            tails,
            lax.dynamic_index_in_dim(blocked, order[k - 1], 0, keepdims=False)[tok - 1],
            order[k],
            0,
        )
    previous = jnp.concatenate([tails[:, None], blocked[:, :-1]], axis=1).reshape(state.shape)
    in_raw = rounded(proj[:, :channels])
    forget_sig = jax.nn.sigmoid(rounded(proj[:, channels : 2 * channels]))
    forget = bound + (1.0 - bound) * forget_sig
    grad_in_raw = carried * (1.0 - forget) * silu_slope(in_raw)
    grad_forget_raw = (
        carried
        * (previous - jax.nn.silu(in_raw))
        * (1.0 - bound)
        * forget_sig
        * (1.0 - forget_sig)
    )
    grad_proj = jnp.concatenate([grad_in_raw, grad_forget_raw, grad_gate], axis=1).astype(bf16)
    in_part = contract(normed, grad_proj, 0, 0).astype(bf16)
    in_held = lax.psum_scatter(in_part, OWNERS, scatter_dimension=0, tiled=True)
    grad_normed = feature_swap(scatter_plane(contract(grad_proj, in_b, 1, 1)), cores, plane)
    grad_gain_one = jnp.sum(grad_normed * unit_one, axis=0)
    weighted_one = grad_normed * gain_f[0]
    grad_block = grad_resid + scale_one * (
        weighted_one - unit_one * jnp.mean(weighted_one * unit_one, axis=1, keepdims=True)
    )

    glu_grad = (
        exchange_plane(glu_held.reshape(plane, rows, 2 * hidden_width))
        .reshape(plane, rows, 2, line, hidden_rows)
        .transpose(1, 2, 3, 0, 4)
        .reshape(glu_w.shape)
        .astype(f32)
    )
    in_grad = (
        exchange_plane(in_held.reshape(plane, rows, 3 * channels))
        .reshape(plane, rows, 3, line, chan)
        .transpose(1, 2, 3, 0, 4)
        .reshape(in_w.shape)
        .astype(f32)
    )
    out_grad = out_grad.astype(f32)
    down_grad = down_grad.astype(f32)

    mid_row = lax.dynamic_update_index_in_dim(
        jnp.zeros((line, plane, chan), f32), grad_gain_mid.reshape(line, chan), rank, 1
    ).reshape(width)
    everyone = (CORE, "x", "y", LINE)
    gain_total = total_small(jnp.stack([grad_gain_one, mid_row, grad_gain_two]), everyone)
    squares = total_small(
        squared(glu_held) + squared(down_grad) + squared(out_grad) + squared(in_held), everyone
    ) + squared(gain_total)
    columns = gains.shape[1]
    gain_grad = lax.dynamic_slice_in_dim(
        gain_total, (device * cores + lax.axis_index(CORE)) * columns, columns, 1
    )
    grad_norm = jnp.sqrt(squares)
    factor = jnp.minimum(1.0, CLIP_LIMIT / (grad_norm + 1e-06))
    in_res = adam_step(in_w, in_m, in_v, in_grad, factor, MATRIX_RATE, MATRIX_DECAY)
    out_res = adam_step(out_w, out_m, out_v, out_grad, factor, MATRIX_RATE, MATRIX_DECAY)
    glu_res = adam_step(glu_w, glu_m, glu_v, glu_grad, factor, MATRIX_RATE, MATRIX_DECAY)
    down_res = adam_step(down_w, down_m, down_v, down_grad, factor, MATRIX_RATE, MATRIX_DECAY)
    gain_res = adam_step(gains, gain_m, gain_v, gain_grad, factor, GAIN_RATE, 0.0)
    return (
        block_out,
        grad_block[None],
        in_res[2],
        out_res[2],
        glu_res[2],
        down_res[2],
        gain_res[2],
        in_res[0],
        out_res[0],
        glu_res[0],
        down_res[0],
        gain_res[0],
        in_res[1],
        out_res[1],
        glu_res[1],
        down_res[1],
        gain_res[1],
        grad_norm,
    )


def split_mesh(mesh):
    seq, cores = mesh.shape["seq"], mesh.shape["rep"]
    side = 1
    while (2 * side) ** 3 <= seq:
        side *= 2
    return Mesh(
        mesh.devices.reshape(seq // (side * side), side, side, cores), (LINE,) + PLANE + (CORE,)
    )


def solution(mesh):
    tokens = P(CORE, (LINE,) + PLANE, None)
    matrix = P((LINE,) + PLANE + (CORE,), None)
    vectors = P(None, (LINE,) + PLANE + (CORE,))
    state = (matrix, matrix, matrix, matrix, vectors)
    return jax.shard_map(
        on_device,
        mesh=split_mesh(mesh),
        in_specs=(tokens, tokens, P(), P(), P((LINE,) + PLANE)) + state * 3,
        out_specs=(tokens, tokens) + state * 3 + (P(),),
        check_vma=False,
    )
```

```python
import functools

import jax
import jax.numpy as jnp
import numpy as np
from jax import lax
from jax.experimental import pallas as pl
from jax.experimental.pallas import tpu as pltpu
from jax.sharding import Mesh, PartitionSpec as P

STEP = 10

NORM_EPS = 1e-06
CLIP_LIMIT = 1.0
BETA_FIRST = 0.9
BETA_SECOND = 0.95
ADAM_EPS = 1e-08
MATRIX_RATE = 0.04
GAIN_RATE = 0.4
MATRIX_DECAY = 0.1

LINE = "z"
PLANE = ("y", "x")
CORE = "core"
MIXER_OWNERS = ("z", "core")
GLU_OWNERS = ("y", "x", "core")


def contract(left_side, right_side, left_dim, right_dim):
    return lax.dot_general(
        left_side,
        right_side,
        (((left_dim,), (right_dim,)), ((), ())),
        preferred_element_type=jnp.float32,
    )


def rounded(values):
    return lax.reduce_precision(values, exponent_bits=8, mantissa_bits=7)


def silu_slope(values):
    logistic = jax.nn.sigmoid(values)
    return logistic * (1.0 + values * (1.0 - logistic))


def sequence_weights(domain_ids, domain_weight):
    kinds = domain_weight.shape[0]
    total = domain_ids.shape[0]
    same_kind = (domain_ids[:, None] == domain_ids[None, :]).astype(jnp.float32)
    counts = jnp.sum(same_kind, axis=1)
    onehot = (domain_ids[:, None] == jnp.arange(kinds, dtype=jnp.int32)[None, :]).astype(
        jnp.float32
    )
    chosen = jnp.sum(onehot * domain_weight[None, :], axis=1)
    return chosen * (total / kinds) / counts


def adam_step(weight, first, second_m, grad, factor, rate, decay):
    clipped = grad * factor
    first_new = BETA_FIRST * first + (1.0 - BETA_FIRST) * clipped
    second_new = BETA_SECOND * second_m + (1.0 - BETA_SECOND) * clipped * clipped
    first_hat = first_new / (1.0 - BETA_FIRST**STEP)
    second_hat = second_new / (1.0 - BETA_SECOND**STEP)
    weight_new = weight - rate * (first_hat / (jnp.sqrt(second_hat) + ADAM_EPS) + decay * weight)
    return (first_new, second_new, weight_new)


def squared(values):
    values = values.astype(jnp.float32)
    return jnp.sum(values * values)


def swap(values, axis, bit):
    size = lax.axis_size(axis)
    return lax.ppermute(values, axis, [(i, i ^ bit) for i in range(size)])


def gather_small(values, axis):
    size = lax.axis_size(axis)
    held = lax.dynamic_update_index_in_dim(
        jnp.zeros((size,) + values.shape, values.dtype), values, lax.axis_index(axis), 0
    )
    bit = 1
    while bit < size:
        held = held + swap(held, axis, bit)
        bit *= 2
    return held


def total_small(values, groups):
    for axes in groups:
        terms = [values] + [swap(values, axes, k) for k in range(1, lax.axis_size(axes))]
        while len(terms) > 1:
            terms = [terms[i] + terms[i + 1] for i in range(0, len(terms), 2)]
        values = terms[0]
    return values


def gather_near(values, axes):
    size = lax.axis_size(axes)
    direct = [k for k in range(1, size) if axes != LINE or k & (k - 1) == 0]
    return {0: values} | {k: swap(values, axes, k) for k in direct}


def gather_far(blocks, axes):
    blocks = dict(blocks)
    for k in range(1, lax.axis_size(axes)):
        if k not in blocks:
            blocks[k] = swap(blocks[k ^ (k & -k)], axes, k & -k)
    return [blocks[k] for k in range(lax.axis_size(axes))]


def gather_tokens(values, axes):
    return jnp.concatenate(gather_far(gather_near(values, axes), axes), axis=0)


def scatter_far(partial, axes):
    size = lax.axis_size(axes)
    rows = partial.shape[0] // size
    blocks = {k: partial[k * rows : (k + 1) * rows] for k in range(size)}
    for k in range(size - 1, 0, -1):
        if axes == LINE and k & (k - 1):
            near = k & -k
            moved = swap(blocks.pop(k).astype(jnp.bfloat16), axes, near)
            blocks[k ^ near] = blocks[k ^ near] + moved.astype(jnp.float32)
    return blocks


def scatter_near(blocks, axes):
    total = blocks[0]
    for k in sorted(blocks, reverse=True)[:-1]:
        total = total + swap(blocks[k].astype(jnp.bfloat16), axes, k).astype(jnp.float32)
    return total


def scatter_tokens(partial, axes):
    return scatter_near(scatter_far(partial, axes), axes)


def total_tokens(values, axes):
    size = lax.axis_size(axes)
    blocks = values.reshape(size, values.shape[0] // size)
    bit = 1
    while bit < size:
        other = swap(blocks, axes, bit)
        blocks = blocks + jnp.stack([other[k ^ bit] for k in range(size)])
        bit *= 2
    return blocks.reshape(values.shape)


def core_sums(part, axes):
    size, cores = lax.axis_size(axes), lax.axis_size(CORE)
    core = lax.axis_index(CORE)
    blocks = part.reshape(size, cores, part.shape[0] // (size * cores), part.shape[1])
    total = lax.dynamic_index_in_dim(blocks, core, 1, keepdims=False).astype(jnp.float32)
    for k in range(1, cores):
        sent = lax.dynamic_index_in_dim(blocks, core ^ k, 1, keepdims=False)
        total = total + swap(sent, CORE, k).astype(jnp.float32)
    return total.astype(jnp.bfloat16)


def rank_sums(blocks, axes):
    rank = lax.axis_index(axes)
    total = lax.dynamic_index_in_dim(blocks, rank, 0, keepdims=False).astype(jnp.float32)
    for k in range(1, lax.axis_size(axes)):
        sent = lax.dynamic_index_in_dim(blocks, rank ^ k, 0, keepdims=False)
        total = total + swap(sent, axes, k).astype(jnp.float32)
    return total


def in_order(blocks, axes):
    rank = lax.axis_index(axes)
    blocks = jnp.stack(blocks)
    return jnp.concatenate(
        [lax.dynamic_index_in_dim(blocks, rank ^ k, 0) for k in range(blocks.shape[0])], axis=0
    )


def core_pair(values):
    return in_order([values] + [swap(values, CORE, k) for k in range(1, lax.axis_size(CORE))], CORE)


def send_each(blocks, axes):
    return [blocks[0]] + [swap(blocks[k], axes, k) for k in range(1, len(blocks))]


def rank_blocks(blocks, axes):
    rank = lax.axis_index(axes)
    return [
        lax.dynamic_index_in_dim(blocks, rank ^ k, 0, keepdims=False)
        for k in range(blocks.shape[0])
    ]


def together(*values):
    return lax.optimization_barrier(values)


def split_kernel(groups, order_ref, values_ref, out_ref):
    count, _, held = out_ref.shape
    unit = held // groups
    for k in range(count):
        for g in range(groups):
            start = pl.multiple_of((g * count + order_ref[k]) * unit, unit)
            out_ref[k, :, g * unit : (g + 1) * unit] = values_ref[:, pl.ds(start, unit)].astype(
                out_ref.dtype
            )


def split_columns(values, groups, order):
    count = order.shape[0]
    rows, width = values.shape
    unit = width // (groups * count)
    if unit % 128:
        blocks = values.astype(jnp.bfloat16).reshape(rows, groups, count, unit)
        blocks = blocks.transpose(2, 0, 1, 3).reshape(count, rows, groups * unit)
        return jnp.stack(
            [lax.dynamic_index_in_dim(blocks, order[k], 0, keepdims=False) for k in range(count)]
        )
    vmem = pl.BlockSpec(memory_space=pltpu.VMEM)
    return pl.pallas_call(
        functools.partial(split_kernel, groups),
        out_shape=jax.ShapeDtypeStruct((count, rows, groups * unit), jnp.bfloat16),
        in_specs=[pl.BlockSpec(memory_space=pltpu.SMEM), vmem],
        out_specs=vmem,
        compiler_params=pltpu.CompilerParams(vmem_limit_bytes=32 * 1024 * 1024),
    )(order, values)


TILE = 8


def gates(proj_ref, rows, width, bound):
    in_raw = proj_ref[rows, 0:width].astype(jnp.bfloat16).astype(jnp.float32)
    forget_raw = proj_ref[rows, width : 2 * width].astype(jnp.bfloat16).astype(jnp.float32)
    forget = bound + (1.0 - bound) * jax.nn.sigmoid(forget_raw)
    return in_raw, forget


def scan_kernel(width, order_ref, proj_ref, bound_ref, state_ref, prod_ref, last_ref):
    blocks = order_ref.shape[0]
    per_block = proj_ref.shape[0] // blocks // TILE
    bound = bound_ref[0:1, :]
    row = lax.broadcasted_iota(jnp.int32, (TILE, width), 0)

    def step(index, carry):
        state_in, prod_in = carry
        tile = order_ref[index // per_block] * per_block + index % per_block
        rows = pl.ds(pl.multiple_of(tile * TILE, TILE), TILE)
        in_raw, forget = gates(proj_ref, rows, width, bound)
        drive = in_raw * jax.nn.sigmoid(in_raw) * (1.0 - forget)
        for shift in (1, 2, 4):
            keep = row >= shift
            drive = jnp.where(keep, forget * pltpu.roll(drive, shift, 0) + drive, drive)
            forget = jnp.where(keep, forget * pltpu.roll(forget, shift, 0), forget)
        state = drive + forget * state_in
        prod = forget * prod_in
        state_ref[rows, :] = state
        prod_ref[rows, :] = prod
        return state[TILE - 1 : TILE, :], prod[TILE - 1 : TILE, :]

    state, prod = lax.fori_loop(
        0,
        blocks * per_block,
        step,
        (jnp.zeros((1, width), jnp.float32), jnp.ones((1, width), jnp.float32)),
    )
    last_ref[0:1, :] = state
    last_ref[1:2, :] = prod


def back_kernel(width, order_ref, proj_ref, bound_ref, grad_ref, carried_ref, prod_ref, last_ref):
    blocks = order_ref.shape[0]
    per_block = proj_ref.shape[0] // blocks // TILE
    count = blocks * per_block
    bound = bound_ref[0:1, :]
    row = lax.broadcasted_iota(jnp.int32, (TILE, width), 0)

    def step(back, carry):
        carried_in, prod_in, forget_next = carry
        index = count - 1 - back
        tile = order_ref[index // per_block] * per_block + index % per_block
        rows = pl.ds(pl.multiple_of(tile * TILE, TILE), TILE)
        _, forget = gates(proj_ref, rows, width, bound)
        rate = jnp.where(row < TILE - 1, pltpu.roll(forget, TILE - 1, 0), forget_next)
        carried = grad_ref[rows, :].astype(jnp.float32)
        for shift in (1, 2, 4):
            keep = row < TILE - shift
            carried = jnp.where(
                keep, rate * pltpu.roll(carried, TILE - shift, 0) + carried, carried
            )
            rate = jnp.where(keep, rate * pltpu.roll(rate, TILE - shift, 0), rate)
        carried = carried + rate * carried_in
        prod = rate * prod_in
        carried_ref[rows, :] = carried
        prod_ref[rows, :] = prod
        return carried[0:1, :], prod[0:1, :], forget[0:1, :]

    ones = jnp.ones((1, width), jnp.float32)
    carried, prod, forget = lax.fori_loop(
        0, count, step, (jnp.zeros((1, width), jnp.float32), ones, ones)
    )
    last_ref[0:1, :] = forget * carried
    last_ref[1:2, :] = forget * prod


def call_scan(kernel, order, *arrays):
    tokens = arrays[0].shape[0]
    width = arrays[1].shape[1]
    vmem = pl.BlockSpec(memory_space=pltpu.VMEM)
    full = jax.ShapeDtypeStruct((tokens, width), jnp.float32)
    return pl.pallas_call(
        functools.partial(kernel, width),
        out_shape=(full, full, jax.ShapeDtypeStruct((2, width), jnp.float32)),
        in_specs=[pl.BlockSpec(memory_space=pltpu.SMEM)] + [vmem] * len(arrays),
        out_specs=(vmem, vmem, vmem),
        compiler_params=pltpu.CompilerParams(vmem_limit_bytes=32 * 1024 * 1024),
    )(order, *arrays)


def on_device(
    block_in,
    cotangent,
    domain_ids,
    domain_weight,
    lower_bound,
    in_w,
    out_w,
    glu_w,
    down_w,
    gains,
    in_m,
    out_m,
    glu_m,
    down_m,
    gain_m,
    in_v,
    out_v,
    glu_v,
    down_v,
    gain_v,
):
    bf16 = jnp.bfloat16
    f32 = jnp.float32
    inputs_f = block_in[0].astype(f32)
    tok, width = inputs_f.shape
    line = lax.axis_size(LINE)
    plane = lax.axis_size(PLANE)
    cores = lax.axis_size(CORE)
    level = lax.axis_index(LINE)
    rank = lax.axis_index(PLANE)
    device = lax.axis_index((LINE,) + PLANE)
    order = jnp.arange(plane, dtype=jnp.int32) ^ rank
    group_seqs = domain_ids.shape[0] // cores
    assert group_seqs == 1
    span = tok * line * plane
    rows = in_w.shape[0]
    chan = lower_bound.shape[0]
    channels = chan * line
    hidden_width = down_w.shape[0] * plane * cores

    seq_scale = sequence_weights(domain_ids, domain_weight)
    position = device * tok + jnp.arange(tok, dtype=jnp.int32)
    owner_seq = lax.axis_index(CORE) * group_seqs + position // (span // group_seqs)
    pick = (owner_seq[:, None] == jnp.arange(domain_ids.shape[0], dtype=jnp.int32)[None, :]).astype(
        f32
    )
    row_weight = jnp.sum(pick * seq_scale[None, :], axis=1)

    def feature_swap(values, outer, inner):
        count = values.shape[0]
        return (
            values.reshape(count, line, outer, inner, rows)
            .transpose(0, 1, 3, 2, 4)
            .reshape(count, width)
        )

    line_order = jnp.arange(line, dtype=jnp.int32) ^ level
    glu_came = send_each(split_columns(glu_w, 2, line_order), LINE)
    glu_held = in_order(glu_came, LINE).reshape(line * rows, 2 * hidden_width)
    in_came = send_each(split_columns(in_w, 3 * line, order), PLANE)
    in_held = in_order(in_came, PLANE).reshape(plane * rows, 3 * channels)

    gain_size = 3 * gains.shape[1]
    packed = jnp.concatenate([rounded(gains).reshape(-1), lower_bound])
    packed = gather_small(packed, LINE)
    bound = packed[:, gain_size:].reshape(1, channels)
    held_gains = gather_small(packed[:, :gain_size], CORE)
    gain_mid = (
        held_gains.reshape(cores, line, 3, gains.shape[1])[:, :, 1]
        .transpose(1, 0, 2)
        .reshape(1, channels)
    )
    held_gains = gather_small(gather_small(held_gains, "x"), "y")
    gain_f = (
        held_gains.reshape(plane, cores, line, 3, gains.shape[1])
        .transpose(3, 2, 0, 1, 4)
        .reshape(3, width)
    )

    in_held, glu_held = together(in_held, glu_held)
    in_b = lax.all_gather(in_held, MIXER_OWNERS, axis=0, tiled=True)

    scale_one = lax.rsqrt(jnp.mean(inputs_f * inputs_f, axis=1, keepdims=True) + NORM_EPS)
    unit_one = inputs_f * scale_one
    normed = feature_swap((unit_one * gain_f[0]).astype(bf16), plane, cores)
    normed = gather_tokens(normed, PLANE)
    proj = contract(normed, in_b, 1, 0)

    glu_held, proj = together(glu_held, proj)
    glu_rows = lax.all_gather(glu_held, GLU_OWNERS, axis=0, tiled=False)
    out_pair = core_pair(out_w.astype(bf16))
    out_blocks = gather_near(out_pair, LINE)
    proj, out_blocks = together(proj, out_blocks)
    out_blocks = gather_far(out_blocks, LINE)
    local_state, local_prod, last = call_scan(scan_kernel, order, proj, bound)
    lasts = gather_small(last, LINE)
    lasts, out_blocks = together(lasts, out_blocks)
    state_in = jnp.zeros((channels,), f32)
    for k in range(line):
        state_in = jnp.where(k < level, lasts[k, 1] * state_in + lasts[k, 0], state_in)
    state = local_state + local_prod * state_in[None, :]
    state_f = rounded(state)
    square_mid = total_tokens(jnp.sum(state_f * state_f, axis=1), PLANE)
    out_b = in_order(out_blocks, LINE).reshape(channels, width)
    scale_mid = lax.rsqrt(square_mid / width + NORM_EPS)[:, None]
    unit_mid = state_f * scale_mid
    gate_raw = proj[:, 2 * channels :]
    gate_act = jax.nn.silu(gate_raw)
    gated = (unit_mid * gain_mid * gate_act).astype(bf16)
    grad_output = cotangent[0].astype(f32) * row_weight[:, None]
    gated, grad_output_b = together(gated, grad_output.astype(bf16))
    grad_output_b = gather_near(grad_output_b, LINE)
    mixed = scatter_tokens(contract(gated, out_b, 1, 0), PLANE)
    mixed, grad_output_b = together(mixed, grad_output_b)
    resid = inputs_f + mixed

    scale_two = lax.rsqrt(jnp.mean(resid * resid, axis=1, keepdims=True) + NORM_EPS)
    unit_two = resid * scale_two
    second_own = (unit_two * gain_f[2]).astype(bf16)
    second_own, down_own, glu_rows = together(second_own, down_w.astype(bf16), glu_rows)
    down_b = lax.all_gather(down_own, GLU_OWNERS, axis=0, tiled=True)
    glu_b = (
        glu_rows.reshape(plane * cores, line, rows, 2 * hidden_width)
        .transpose(1, 0, 2, 3)
        .reshape(width, 2 * hidden_width)
    )
    second, glu_b = together(gather_near(second_own, LINE), glu_b)
    second = jnp.concatenate(gather_far(second, LINE), axis=0)
    second, grad_output_b = together(second, grad_output_b)
    paired = contract(second, glu_b, 1, 0)
    up_gate = paired[:, :hidden_width]
    up_value = paired[:, hidden_width:]
    gate_silu = jax.nn.silu(up_gate)
    hidden = (gate_silu * up_value).astype(bf16)

    grad_output_b = jnp.concatenate(gather_far(grad_output_b, LINE), axis=0)
    grad_hidden = contract(grad_output_b, down_b, 1, 1)
    grad_paired = jnp.concatenate(
        [grad_hidden * up_value * silu_slope(up_gate), grad_hidden * gate_silu], axis=1
    ).astype(bf16)
    second_part = contract(grad_paired, glu_b, 1, 1)
    grad_second = scatter_tokens(second_part, LINE)
    owned = (
        second
        .reshape(line * tok, line, plane * cores, rows)
        .transpose(0, 2, 1, 3)
        .reshape(line * tok, width)
    )
    glu_part = contract(owned, grad_paired, 0, 0).astype(bf16)
    glu_held = lax.psum_scatter(glu_part, GLU_OWNERS, scatter_dimension=0, tiled=True)
    down_part = contract(hidden, grad_output_b, 0, 0).astype(bf16)
    down_sums = core_sums(down_part, PLANE)
    grad_gain_two = jnp.sum(grad_second * unit_two, axis=0)
    weighted_two = grad_second * gain_f[2]
    grad_resid = grad_output + scale_two * (
        weighted_two - unit_two * jnp.mean(weighted_two * unit_two, axis=1, keepdims=True)
    )

    grad_resid, hidden = together(grad_resid, hidden)
    output = resid + scatter_tokens(contract(hidden, down_b, 1, 0), LINE)
    block_out = output.astype(bf16)[None]

    grad_resid_b = gather_tokens(grad_resid.astype(bf16), PLANE)
    grad_resid_b, block_out = together(grad_resid_b, block_out)
    grad_gated = contract(grad_resid_b, out_b, 1, 1)
    out_part = contract(gated, grad_resid_b, 0, 0).astype(bf16)
    grad_gain_mid = jnp.sum(grad_gated * unit_mid * gate_act, axis=0)
    grad_gate = grad_gated * unit_mid * gain_mid * silu_slope(gate_raw)
    weighted_mid = grad_gated * gain_mid * gate_act
    mean_mid = total_tokens(jnp.sum(weighted_mid * unit_mid, axis=1), PLANE) / width
    out_part, glu_held = together(out_part, glu_held)
    out_grad = lax.psum_scatter(out_part, MIXER_OWNERS, scatter_dimension=0, tiled=True)
    grad_state = scale_mid * (weighted_mid - unit_mid * mean_mid[:, None])
    local_carried, local_rate, first = call_scan(
        back_kernel, order, proj, bound, rounded(grad_state)
    )
    firsts = gather_small(first, LINE)
    carried_in = jnp.zeros((channels,), f32)
    for k in range(line - 1, -1, -1):
        carried_in = jnp.where(k > level, firsts[k, 1] * carried_in + firsts[k, 0], carried_in)
    carried = local_carried + local_rate * carried_in[None, :]
    blocked = state.reshape(plane, tok, channels)
    tails = lax.dynamic_update_index_in_dim(
        jnp.zeros((plane, channels), f32), state_in, order[0], 0
    )
    for k in range(1, plane):
        tails = lax.dynamic_update_index_in_dim(
            tails,
            lax.dynamic_index_in_dim(blocked, order[k - 1], 0, keepdims=False)[tok - 1],
            order[k],
            0,
        )
    previous = jnp.concatenate([tails[:, None], blocked[:, :-1]], axis=1).reshape(state.shape)
    in_raw = rounded(proj[:, :channels])
    forget_sig = jax.nn.sigmoid(rounded(proj[:, channels : 2 * channels]))
    forget = bound + (1.0 - bound) * forget_sig
    grad_in_raw = carried * (1.0 - forget) * silu_slope(in_raw)
    grad_forget_raw = (
        carried
        * (previous - jax.nn.silu(in_raw))
        * (1.0 - bound)
        * forget_sig
        * (1.0 - forget_sig)
    )
    grad_proj = jnp.concatenate([grad_in_raw, grad_forget_raw, grad_gate], axis=1).astype(bf16)
    in_part = contract(normed, grad_proj, 0, 0).astype(bf16)
    in_held = lax.psum_scatter(in_part, MIXER_OWNERS, scatter_dimension=0, tiled=True)
    down_grad = rank_sums(down_sums, PLANE)
    grad_normed = feature_swap(
        scatter_tokens(contract(grad_proj, in_b, 1, 1), PLANE), cores, plane
    )
    grad_gain_one = jnp.sum(grad_normed * unit_one, axis=0)
    weighted_one = grad_normed * gain_f[0]
    grad_block = grad_resid + scale_one * (
        weighted_one - unit_one * jnp.mean(weighted_one * unit_one, axis=1, keepdims=True)
    )

    mid_row = lax.dynamic_update_index_in_dim(
        jnp.zeros((line, plane, chan), f32), grad_gain_mid.reshape(line, chan), rank, 1
    ).reshape(width)
    gain_part = jnp.stack([grad_gain_one, mid_row, grad_gain_two])
    early_squares = squared(glu_held) + squared(down_grad) + squared(out_grad)
    glu_sent = rank_blocks(glu_held.reshape(line, rows, 2 * hidden_width), LINE)
    in_held, glu_sent, gain_part, early_squares, grad_block = together(
        in_held, glu_sent, gain_part, early_squares, grad_block
    )
    glu_came = send_each(glu_sent, LINE)
    squares = jnp.broadcast_to(early_squares + squared(in_held), (1, width))
    totals = total_small(
        jnp.concatenate([gain_part, squares], axis=0), (CORE, PLANE, LINE)
    )
    glu_blocks = in_order(glu_came, LINE)
    glu_grad = jnp.concatenate(
        [glu_blocks[q, :, :hidden_width] for q in range(line)]
        + [glu_blocks[q, :, hidden_width:] for q in range(line)],
        axis=1,
    )
    in_blocks = in_held.reshape(plane, rows, 3 * channels)
    in_came = send_each(rank_blocks(in_blocks, PLANE), PLANE)
    in_grad = (
        in_order(in_came, PLANE)
        .reshape(plane, rows, 3, line, chan)
        .transpose(1, 2, 3, 0, 4)
        .reshape(in_w.shape)
    )
    gain_total = totals[:3]
    squares = totals[3, 0] + squared(gain_total)
    in_grad, glu_grad, squares = lax.optimization_barrier((in_grad, glu_grad, squares))
    in_grad, glu_grad, out_grad = (v.astype(f32) for v in (in_grad, glu_grad, out_grad))
    columns = gains.shape[1]
    gain_grad = lax.dynamic_slice_in_dim(
        gain_total, (device * cores + lax.axis_index(CORE)) * columns, columns, 1
    )
    grad_norm = jnp.sqrt(squares)
    factor = jnp.minimum(1.0, CLIP_LIMIT / (grad_norm + 1e-06))
    in_res = adam_step(in_w, in_m, in_v, in_grad, factor, MATRIX_RATE, MATRIX_DECAY)
    out_res = adam_step(out_w, out_m, out_v, out_grad, factor, MATRIX_RATE, MATRIX_DECAY)
    glu_res = adam_step(glu_w, glu_m, glu_v, glu_grad, factor, MATRIX_RATE, MATRIX_DECAY)
    down_res = adam_step(down_w, down_m, down_v, down_grad, factor, MATRIX_RATE, MATRIX_DECAY)
    gain_res = adam_step(gains, gain_m, gain_v, gain_grad, factor, GAIN_RATE, 0.0)
    return (
        block_out,
        grad_block[None],
        in_res[2],
        out_res[2],
        glu_res[2],
        down_res[2],
        gain_res[2],
        in_res[0],
        out_res[0],
        glu_res[0],
        down_res[0],
        gain_res[0],
        in_res[1],
        out_res[1],
        glu_res[1],
        down_res[1],
        gain_res[1],
        grad_norm,
    )


def split_mesh(mesh):
    seq, cores = mesh.shape["seq"], mesh.shape["rep"]
    side = 1
    while (2 * side) ** 3 <= seq:
        side *= 2
    return Mesh(
        mesh.devices.reshape(seq // (side * side), side, side, cores), (LINE,) + PLANE + (CORE,)
    )


def solution(mesh):
    tokens = P(CORE, (LINE,) + PLANE, None)
    matrix = P((LINE,) + PLANE + (CORE,), None)
    vectors = P(None, (LINE,) + PLANE + (CORE,))
    state = (matrix, matrix, matrix, matrix, vectors)
    return jax.shard_map(
        on_device,
        mesh=split_mesh(mesh),
        in_specs=(tokens, tokens, P(), P(), P((LINE,) + PLANE)) + state * 3,
        out_specs=(tokens, tokens) + state * 3 + (P(),),
        check_vma=False,
    )
```

```python
import functools

import jax
import jax.numpy as jnp
import numpy as np
from jax import lax
from jax.experimental import pallas as pl
from jax.experimental.pallas import tpu as pltpu
from jax.sharding import Mesh, PartitionSpec as P

STEP = 10

NORM_EPS = 1e-06
CLIP_LIMIT = 1.0
BETA_FIRST = 0.9
BETA_SECOND = 0.95
ADAM_EPS = 1e-08
MATRIX_RATE = 0.04
GAIN_RATE = 0.4
MATRIX_DECAY = 0.1

LINE = "z"
PLANE = ("y", "x")
CORE = "core"
MIXER_OWNERS = ("z", "core")
GLU_OWNERS = ("y", "x", "core")


def contract(left_side, right_side, left_dim, right_dim):
    return lax.dot_general(
        left_side,
        right_side,
        (((left_dim,), (right_dim,)), ((), ())),
        preferred_element_type=jnp.float32,
    )


def rounded(values):
    return lax.reduce_precision(values, exponent_bits=8, mantissa_bits=7)


def silu_slope(values):
    logistic = jax.nn.sigmoid(values)
    return logistic * (1.0 + values * (1.0 - logistic))


def sequence_weights(domain_ids, domain_weight):
    kinds = domain_weight.shape[0]
    total = domain_ids.shape[0]
    same_kind = (domain_ids[:, None] == domain_ids[None, :]).astype(jnp.float32)
    counts = jnp.sum(same_kind, axis=1)
    onehot = (domain_ids[:, None] == jnp.arange(kinds, dtype=jnp.int32)[None, :]).astype(
        jnp.float32
    )
    chosen = jnp.sum(onehot * domain_weight[None, :], axis=1)
    return chosen * (total / kinds) / counts


def adam_step(weight, first, second_m, grad, factor, rate, decay):
    clipped = grad * factor
    first_new = BETA_FIRST * first + (1.0 - BETA_FIRST) * clipped
    second_new = BETA_SECOND * second_m + (1.0 - BETA_SECOND) * clipped * clipped
    first_hat = first_new / (1.0 - BETA_FIRST**STEP)
    second_hat = second_new / (1.0 - BETA_SECOND**STEP)
    weight_new = weight - rate * (first_hat / (jnp.sqrt(second_hat) + ADAM_EPS) + decay * weight)
    return (first_new, second_new, weight_new)


def squared(values):
    values = values.astype(jnp.float32)
    return jnp.sum(values * values)


def swap(values, axis, bit):
    size = lax.axis_size(axis)
    return lax.ppermute(values, axis, [(i, i ^ bit) for i in range(size)])


def gather_small(values, axis):
    size = lax.axis_size(axis)
    held = lax.dynamic_update_index_in_dim(
        jnp.zeros((size,) + values.shape, values.dtype), values, lax.axis_index(axis), 0
    )
    bit = 1
    while bit < size:
        held = held + swap(held, axis, bit)
        bit *= 2
    return held


def total_small(values, groups):
    for axes in groups:
        terms = [values] + [swap(values, axes, k) for k in range(1, lax.axis_size(axes))]
        while len(terms) > 1:
            terms = [terms[i] + terms[i + 1] for i in range(0, len(terms), 2)]
        values = terms[0]
    return values


def gather_near(values, axes):
    size = lax.axis_size(axes)
    direct = [k for k in range(1, size) if axes != LINE or k & (k - 1) == 0]
    return {0: values} | {k: swap(values, axes, k) for k in direct}


def gather_far(blocks, axes):
    blocks = dict(blocks)
    for k in range(1, lax.axis_size(axes)):
        if k not in blocks:
            blocks[k] = swap(blocks[k ^ (k & -k)], axes, k & -k)
    return [blocks[k] for k in range(lax.axis_size(axes))]


def gather_tokens(values, axes):
    return jnp.concatenate(gather_far(gather_near(values, axes), axes), axis=0)


def scatter_far(partial, axes):
    size = lax.axis_size(axes)
    rows = partial.shape[0] // size
    blocks = {k: partial[k * rows : (k + 1) * rows] for k in range(size)}
    for k in range(size - 1, 0, -1):
        if axes == LINE and k & (k - 1):
            near = k & -k
            moved = swap(blocks.pop(k).astype(jnp.bfloat16), axes, near)
            blocks[k ^ near] = blocks[k ^ near] + moved.astype(jnp.float32)
    return blocks


def scatter_near(blocks, axes):
    total = blocks[0]
    for k in sorted(blocks, reverse=True)[:-1]:
        total = total + swap(blocks[k].astype(jnp.bfloat16), axes, k).astype(jnp.float32)
    return total


def scatter_tokens(partial, axes):
    return scatter_near(scatter_far(partial, axes), axes)


def total_tokens(values, axes):
    size = lax.axis_size(axes)
    blocks = values.reshape(size, values.shape[0] // size)
    bit = 1
    while bit < size:
        other = swap(blocks, axes, bit)
        blocks = blocks + jnp.stack([other[k ^ bit] for k in range(size)])
        bit *= 2
    return blocks.reshape(values.shape)


def core_sums(part, axes):
    size, cores = lax.axis_size(axes), lax.axis_size(CORE)
    core = lax.axis_index(CORE)
    blocks = part.reshape(size, cores, part.shape[0] // (size * cores), part.shape[1])
    total = lax.dynamic_index_in_dim(blocks, core, 1, keepdims=False).astype(jnp.float32)
    for k in range(1, cores):
        sent = lax.dynamic_index_in_dim(blocks, core ^ k, 1, keepdims=False)
        total = total + swap(sent, CORE, k).astype(jnp.float32)
    return total.astype(jnp.bfloat16)


def rank_sums(blocks, axes):
    rank = lax.axis_index(axes)
    total = lax.dynamic_index_in_dim(blocks, rank, 0, keepdims=False).astype(jnp.float32)
    for k in range(1, lax.axis_size(axes)):
        sent = lax.dynamic_index_in_dim(blocks, rank ^ k, 0, keepdims=False)
        total = total + swap(sent, axes, k).astype(jnp.float32)
    return total


def in_order(blocks, axes):
    rank = lax.axis_index(axes)
    blocks = jnp.stack(blocks)
    return jnp.concatenate(
        [lax.dynamic_index_in_dim(blocks, rank ^ k, 0) for k in range(blocks.shape[0])], axis=0
    )


def core_pair(values):
    return in_order([values] + [swap(values, CORE, k) for k in range(1, lax.axis_size(CORE))], CORE)


def send_each(blocks, axes):
    return [blocks[0]] + [swap(blocks[k], axes, k) for k in range(1, len(blocks))]


def rank_blocks(blocks, axes):
    rank = lax.axis_index(axes)
    return [
        lax.dynamic_index_in_dim(blocks, rank ^ k, 0, keepdims=False)
        for k in range(blocks.shape[0])
    ]


def together(*values):
    return lax.optimization_barrier(values)


def split_kernel(groups, order_ref, values_ref, out_ref):
    count, _, held = out_ref.shape
    unit = held // groups
    for k in range(count):
        for g in range(groups):
            start = pl.multiple_of((g * count + order_ref[k]) * unit, unit)
            out_ref[k, :, g * unit : (g + 1) * unit] = values_ref[:, pl.ds(start, unit)].astype(
                out_ref.dtype
            )


def split_columns(values, groups, order):
    count = order.shape[0]
    rows, width = values.shape
    unit = width // (groups * count)
    if unit % 128:
        blocks = values.astype(jnp.bfloat16).reshape(rows, groups, count, unit)
        blocks = blocks.transpose(2, 0, 1, 3).reshape(count, rows, groups * unit)
        return jnp.stack(
            [lax.dynamic_index_in_dim(blocks, order[k], 0, keepdims=False) for k in range(count)]
        )
    vmem = pl.BlockSpec(memory_space=pltpu.VMEM)
    return pl.pallas_call(
        functools.partial(split_kernel, groups),
        out_shape=jax.ShapeDtypeStruct((count, rows, groups * unit), jnp.bfloat16),
        in_specs=[pl.BlockSpec(memory_space=pltpu.SMEM), vmem],
        out_specs=vmem,
        compiler_params=pltpu.CompilerParams(vmem_limit_bytes=32 * 1024 * 1024),
    )(order, values)


def join_kernel(groups, order_ref, *refs):
    *came_refs, out_ref = refs
    count = len(came_refs)
    unit = out_ref.shape[1] // (groups * count)
    for k, came_ref in enumerate(came_refs):
        for g in range(groups):
            start = pl.multiple_of((g * count + order_ref[k]) * unit, unit)
            out_ref[:, pl.ds(start, unit)] = came_ref[:, g * unit : (g + 1) * unit]


def join_columns(came, groups, order, axes):
    rows, held = came[0].shape
    unit = held // groups
    if unit % 128:
        blocks = in_order(came, axes)
        return jnp.concatenate(
            [block[:, g * unit : (g + 1) * unit] for g in range(groups) for block in blocks], axis=1
        )
    vmem = pl.BlockSpec(memory_space=pltpu.VMEM)
    return pl.pallas_call(
        functools.partial(join_kernel, groups),
        out_shape=jax.ShapeDtypeStruct((rows, held * len(came)), came[0].dtype),
        in_specs=[pl.BlockSpec(memory_space=pltpu.SMEM)] + [vmem] * len(came),
        out_specs=vmem,
        compiler_params=pltpu.CompilerParams(vmem_limit_bytes=32 * 1024 * 1024),
    )(order, *came)


def turn_kernel(groups, outer, inner, values_ref, out_ref):
    unit = out_ref.shape[1] // (groups * outer * inner)
    for g in range(groups):
        for i in range(outer):
            for j in range(inner):
                old, new = (g * outer + i) * inner + j, (g * inner + j) * outer + i
                out_ref[:, new * unit : (new + 1) * unit] = values_ref[
                    :, old * unit : (old + 1) * unit
                ].astype(out_ref.dtype)


def turn_columns(values, groups, outer, inner, dtype):
    rows, width = values.shape
    unit = width // (groups * outer * inner)
    if unit % 64:
        values = values.astype(dtype).reshape(rows, groups, outer, inner, unit)
        return values.transpose(0, 1, 3, 2, 4).reshape(rows, width)
    vmem = pl.BlockSpec(memory_space=pltpu.VMEM)
    return pl.pallas_call(
        functools.partial(turn_kernel, groups, outer, inner),
        out_shape=jax.ShapeDtypeStruct((rows, width), dtype),
        in_specs=[vmem],
        out_specs=vmem,
        compiler_params=pltpu.CompilerParams(vmem_limit_bytes=32 * 1024 * 1024),
    )(values)


TILE = 8


def gates(proj_ref, rows, width, bound):
    in_raw = proj_ref[rows, 0:width].astype(jnp.bfloat16).astype(jnp.float32)
    forget_raw = proj_ref[rows, width : 2 * width].astype(jnp.bfloat16).astype(jnp.float32)
    forget = bound + (1.0 - bound) * jax.nn.sigmoid(forget_raw)
    return in_raw, forget


def scan_kernel(width, order_ref, proj_ref, bound_ref, state_ref, prod_ref, last_ref):
    blocks = order_ref.shape[0]
    per_block = proj_ref.shape[0] // blocks // TILE
    bound = bound_ref[0:1, :]
    row = lax.broadcasted_iota(jnp.int32, (TILE, width), 0)

    def step(index, carry):
        state_in, prod_in = carry
        tile = order_ref[index // per_block] * per_block + index % per_block
        rows = pl.ds(pl.multiple_of(tile * TILE, TILE), TILE)
        in_raw, forget = gates(proj_ref, rows, width, bound)
        drive = in_raw * jax.nn.sigmoid(in_raw) * (1.0 - forget)
        for shift in (1, 2, 4):
            keep = row >= shift
            drive = jnp.where(keep, forget * pltpu.roll(drive, shift, 0) + drive, drive)
            forget = jnp.where(keep, forget * pltpu.roll(forget, shift, 0), forget)
        state = drive + forget * state_in
        prod = forget * prod_in
        state_ref[rows, :] = state
        prod_ref[rows, :] = prod
        return state[TILE - 1 : TILE, :], prod[TILE - 1 : TILE, :]

    state, prod = lax.fori_loop(
        0,
        blocks * per_block,
        step,
        (jnp.zeros((1, width), jnp.float32), jnp.ones((1, width), jnp.float32)),
    )
    last_ref[0:1, :] = state
    last_ref[1:2, :] = prod


def back_kernel(width, order_ref, proj_ref, bound_ref, grad_ref, carried_ref, prod_ref, last_ref):
    blocks = order_ref.shape[0]
    per_block = proj_ref.shape[0] // blocks // TILE
    count = blocks * per_block
    bound = bound_ref[0:1, :]
    row = lax.broadcasted_iota(jnp.int32, (TILE, width), 0)

    def step(back, carry):
        carried_in, prod_in, forget_next = carry
        index = count - 1 - back
        tile = order_ref[index // per_block] * per_block + index % per_block
        rows = pl.ds(pl.multiple_of(tile * TILE, TILE), TILE)
        _, forget = gates(proj_ref, rows, width, bound)
        rate = jnp.where(row < TILE - 1, pltpu.roll(forget, TILE - 1, 0), forget_next)
        carried = grad_ref[rows, :].astype(jnp.float32)
        for shift in (1, 2, 4):
            keep = row < TILE - shift
            carried = jnp.where(
                keep, rate * pltpu.roll(carried, TILE - shift, 0) + carried, carried
            )
            rate = jnp.where(keep, rate * pltpu.roll(rate, TILE - shift, 0), rate)
        carried = carried + rate * carried_in
        prod = rate * prod_in
        carried_ref[rows, :] = carried
        prod_ref[rows, :] = prod
        return carried[0:1, :], prod[0:1, :], forget[0:1, :]

    ones = jnp.ones((1, width), jnp.float32)
    carried, prod, forget = lax.fori_loop(
        0, count, step, (jnp.zeros((1, width), jnp.float32), ones, ones)
    )
    last_ref[0:1, :] = forget * carried
    last_ref[1:2, :] = forget * prod


def call_scan(kernel, order, *arrays):
    tokens = arrays[0].shape[0]
    width = arrays[1].shape[1]
    vmem = pl.BlockSpec(memory_space=pltpu.VMEM)
    full = jax.ShapeDtypeStruct((tokens, width), jnp.float32)
    return pl.pallas_call(
        functools.partial(kernel, width),
        out_shape=(full, full, jax.ShapeDtypeStruct((2, width), jnp.float32)),
        in_specs=[pl.BlockSpec(memory_space=pltpu.SMEM)] + [vmem] * len(arrays),
        out_specs=(vmem, vmem, vmem),
        compiler_params=pltpu.CompilerParams(vmem_limit_bytes=32 * 1024 * 1024),
    )(order, *arrays)


def on_device(
    block_in,
    cotangent,
    domain_ids,
    domain_weight,
    lower_bound,
    in_w,
    out_w,
    glu_w,
    down_w,
    gains,
    in_m,
    out_m,
    glu_m,
    down_m,
    gain_m,
    in_v,
    out_v,
    glu_v,
    down_v,
    gain_v,
):
    bf16 = jnp.bfloat16
    f32 = jnp.float32
    inputs_f = block_in[0].astype(f32)
    tok, width = inputs_f.shape
    line = lax.axis_size(LINE)
    plane = lax.axis_size(PLANE)
    cores = lax.axis_size(CORE)
    level = lax.axis_index(LINE)
    rank = lax.axis_index(PLANE)
    device = lax.axis_index((LINE,) + PLANE)
    order = jnp.arange(plane, dtype=jnp.int32) ^ rank
    group_seqs = domain_ids.shape[0] // cores
    assert group_seqs == 1
    span = tok * line * plane
    rows = in_w.shape[0]
    chan = lower_bound.shape[0]
    channels = chan * line
    hidden_width = down_w.shape[0] * plane * cores

    seq_scale = sequence_weights(domain_ids, domain_weight)
    position = device * tok + jnp.arange(tok, dtype=jnp.int32)
    owner_seq = lax.axis_index(CORE) * group_seqs + position // (span // group_seqs)
    pick = (owner_seq[:, None] == jnp.arange(domain_ids.shape[0], dtype=jnp.int32)[None, :]).astype(
        f32
    )
    row_weight = jnp.sum(pick * seq_scale[None, :], axis=1)


    line_order = jnp.arange(line, dtype=jnp.int32) ^ level
    glu_came = send_each(split_columns(glu_w, 2, line_order), LINE)
    glu_held = in_order(glu_came, LINE).reshape(line * rows, 2 * hidden_width)
    in_came = send_each(split_columns(in_w, 3 * line, order), PLANE)
    in_held = in_order(in_came, PLANE).reshape(plane * rows, 3 * channels)

    gain_size = 3 * gains.shape[1]
    packed = jnp.concatenate([rounded(gains).reshape(-1), lower_bound])
    packed = gather_small(packed, LINE)
    bound = packed[:, gain_size:].reshape(1, channels)
    held_gains = gather_small(packed[:, :gain_size], CORE)
    gain_mid = (
        held_gains.reshape(cores, line, 3, gains.shape[1])[:, :, 1]
        .transpose(1, 0, 2)
        .reshape(1, channels)
    )
    held_gains = gather_small(gather_small(held_gains, "x"), "y")
    gain_f = (
        held_gains.reshape(plane, cores, line, 3, gains.shape[1])
        .transpose(3, 2, 0, 1, 4)
        .reshape(3, width)
    )

    in_held, glu_held = together(in_held, glu_held)
    in_b = lax.all_gather(in_held, MIXER_OWNERS, axis=0, tiled=True)

    scale_one = lax.rsqrt(jnp.mean(inputs_f * inputs_f, axis=1, keepdims=True) + NORM_EPS)
    unit_one = inputs_f * scale_one
    normed = turn_columns(unit_one * gain_f[0], line, plane, cores, bf16)
    normed = gather_tokens(normed, PLANE)
    proj = contract(normed, in_b, 1, 0)

    glu_held, proj = together(glu_held, proj)
    glu_b = lax.all_gather(glu_held, GLU_OWNERS, axis=0, tiled=True)
    out_pair = core_pair(out_w.astype(bf16))
    out_blocks = gather_near(out_pair, LINE)
    proj, out_blocks = together(proj, out_blocks)
    out_blocks = gather_far(out_blocks, LINE)
    local_state, local_prod, last = call_scan(scan_kernel, order, proj, bound)
    lasts = gather_small(last, LINE)
    lasts, out_blocks = together(lasts, out_blocks)
    state_in = jnp.zeros((channels,), f32)
    for k in range(line):
        state_in = jnp.where(k < level, lasts[k, 1] * state_in + lasts[k, 0], state_in)
    state = local_state + local_prod * state_in[None, :]
    state_f = rounded(state)
    square_mid = total_tokens(jnp.sum(state_f * state_f, axis=1), PLANE)
    out_b = in_order(out_blocks, LINE).reshape(channels, width)
    scale_mid = lax.rsqrt(square_mid / width + NORM_EPS)[:, None]
    unit_mid = state_f * scale_mid
    gate_raw = proj[:, 2 * channels :]
    gate_act = jax.nn.silu(gate_raw)
    gated = (unit_mid * gain_mid * gate_act).astype(bf16)
    grad_output = cotangent[0].astype(f32) * row_weight[:, None]
    gated, grad_output_b = together(gated, grad_output.astype(bf16))
    grad_output_b = gather_near(grad_output_b, LINE)
    mixed = scatter_tokens(contract(gated, out_b, 1, 0), PLANE)
    mixed, grad_output_b = together(mixed, grad_output_b)
    resid = inputs_f + mixed

    scale_two = lax.rsqrt(jnp.mean(resid * resid, axis=1, keepdims=True) + NORM_EPS)
    unit_two = resid * scale_two
    second_own = turn_columns(unit_two * gain_f[2], 1, line, plane * cores, bf16)
    second_own, down_own, glu_b = together(second_own, down_w.astype(bf16), glu_b)
    down_b = lax.all_gather(down_own, GLU_OWNERS, axis=0, tiled=True)
    second, glu_b = together(gather_near(second_own, LINE), glu_b)
    second = jnp.concatenate(gather_far(second, LINE), axis=0)
    second, grad_output_b = together(second, grad_output_b)
    paired = contract(second, glu_b, 1, 0)
    up_gate = paired[:, :hidden_width]
    up_value = paired[:, hidden_width:]
    gate_silu = jax.nn.silu(up_gate)
    hidden = (gate_silu * up_value).astype(bf16)

    grad_output_b = jnp.concatenate(gather_far(grad_output_b, LINE), axis=0)
    grad_hidden = contract(grad_output_b, down_b, 1, 1)
    grad_paired = jnp.concatenate(
        [grad_hidden * up_value * silu_slope(up_gate), grad_hidden * gate_silu], axis=1
    ).astype(bf16)
    second_part = contract(grad_paired, glu_b, 1, 1)
    grad_second = scatter_tokens(second_part, LINE)
    grad_second = turn_columns(grad_second, 1, plane * cores, line, f32)
    glu_part = contract(second, grad_paired, 0, 0).astype(bf16)
    glu_held = lax.psum_scatter(glu_part, GLU_OWNERS, scatter_dimension=0, tiled=True)
    down_part = contract(hidden, grad_output_b, 0, 0).astype(bf16)
    down_sums = core_sums(down_part, PLANE)
    grad_second, down_sums = together(grad_second, down_sums)
    grad_gain_two = jnp.sum(grad_second * unit_two, axis=0)
    weighted_two = grad_second * gain_f[2]
    grad_resid = grad_output + scale_two * (
        weighted_two - unit_two * jnp.mean(weighted_two * unit_two, axis=1, keepdims=True)
    )

    grad_resid, hidden = together(grad_resid, hidden)
    output = resid + scatter_tokens(contract(hidden, down_b, 1, 0), LINE)
    block_out = output.astype(bf16)[None]

    grad_resid_b = gather_tokens(grad_resid.astype(bf16), PLANE)
    grad_resid_b, block_out = together(grad_resid_b, block_out)
    grad_gated = contract(grad_resid_b, out_b, 1, 1)
    out_part = contract(gated, grad_resid_b, 0, 0).astype(bf16)
    grad_gain_mid = jnp.sum(grad_gated * unit_mid * gate_act, axis=0)
    grad_gate = grad_gated * unit_mid * gain_mid * silu_slope(gate_raw)
    weighted_mid = grad_gated * gain_mid * gate_act
    mean_mid = total_tokens(jnp.sum(weighted_mid * unit_mid, axis=1), PLANE) / width
    out_part, glu_held = together(out_part, glu_held)
    out_grad = lax.psum_scatter(out_part, MIXER_OWNERS, scatter_dimension=0, tiled=True)
    grad_state = scale_mid * (weighted_mid - unit_mid * mean_mid[:, None])
    local_carried, local_rate, first = call_scan(
        back_kernel, order, proj, bound, rounded(grad_state)
    )
    firsts = gather_small(first, LINE)
    carried_in = jnp.zeros((channels,), f32)
    for k in range(line - 1, -1, -1):
        carried_in = jnp.where(k > level, firsts[k, 1] * carried_in + firsts[k, 0], carried_in)
    carried = local_carried + local_rate * carried_in[None, :]
    blocked = state.reshape(plane, tok, channels)
    tails = lax.dynamic_update_index_in_dim(
        jnp.zeros((plane, channels), f32), state_in, order[0], 0
    )
    for k in range(1, plane):
        tails = lax.dynamic_update_index_in_dim(
            tails,
            lax.dynamic_index_in_dim(blocked, order[k - 1], 0, keepdims=False)[tok - 1],
            order[k],
            0,
        )
    previous = jnp.concatenate([tails[:, None], blocked[:, :-1]], axis=1).reshape(state.shape)
    in_raw = rounded(proj[:, :channels])
    forget_sig = jax.nn.sigmoid(rounded(proj[:, channels : 2 * channels]))
    forget = bound + (1.0 - bound) * forget_sig
    grad_in_raw = carried * (1.0 - forget) * silu_slope(in_raw)
    grad_forget_raw = (
        carried
        * (previous - jax.nn.silu(in_raw))
        * (1.0 - bound)
        * forget_sig
        * (1.0 - forget_sig)
    )
    grad_proj = jnp.concatenate([grad_in_raw, grad_forget_raw, grad_gate], axis=1).astype(bf16)
    in_part = contract(normed, grad_proj, 0, 0).astype(bf16)
    in_held = lax.psum_scatter(in_part, MIXER_OWNERS, scatter_dimension=0, tiled=True)
    down_grad = rank_sums(down_sums, PLANE)
    grad_normed = scatter_tokens(contract(grad_proj, in_b, 1, 1), PLANE)
    grad_normed = turn_columns(grad_normed, line, cores, plane, f32)
    grad_gain_one = jnp.sum(grad_normed * unit_one, axis=0)
    weighted_one = grad_normed * gain_f[0]
    grad_block = grad_resid + scale_one * (
        weighted_one - unit_one * jnp.mean(weighted_one * unit_one, axis=1, keepdims=True)
    )

    mid_row = lax.dynamic_update_index_in_dim(
        jnp.zeros((line, plane, chan), f32), grad_gain_mid.reshape(line, chan), rank, 1
    ).reshape(width)
    gain_part = jnp.stack([grad_gain_one, mid_row, grad_gain_two])
    early_squares = squared(glu_held) + squared(down_grad) + squared(out_grad)
    glu_sent = rank_blocks(glu_held.reshape(line, rows, 2 * hidden_width), LINE)
    in_held, glu_sent, gain_part, early_squares, grad_block = together(
        in_held, glu_sent, gain_part, early_squares, grad_block
    )
    glu_came = send_each(glu_sent, LINE)
    squares = jnp.broadcast_to(early_squares + squared(in_held), (1, width))
    totals = total_small(
        jnp.concatenate([gain_part, squares], axis=0), (LINE, PLANE, CORE)
    )
    in_blocks = in_held.reshape(plane, rows, 3 * channels)
    in_grad = join_columns(
        send_each(rank_blocks(in_blocks, PLANE), PLANE), 3 * line, order, PLANE
    )
    gain_total = totals[:3]
    squares = totals[3, 0] + squared(gain_total)
    in_grad, squares = together(in_grad, squares)
    in_grad, out_grad = in_grad.astype(f32), out_grad.astype(f32)
    columns = gains.shape[1]
    gain_grad = lax.dynamic_slice_in_dim(
        gain_total, (device * cores + lax.axis_index(CORE)) * columns, columns, 1
    )
    grad_norm = jnp.sqrt(squares)
    factor = jnp.minimum(1.0, CLIP_LIMIT / (grad_norm + 1e-06))
    in_res = adam_step(in_w, in_m, in_v, in_grad, factor, MATRIX_RATE, MATRIX_DECAY)
    out_res = adam_step(out_w, out_m, out_v, out_grad, factor, MATRIX_RATE, MATRIX_DECAY)
    down_res = adam_step(down_w, down_m, down_v, down_grad, factor, MATRIX_RATE, MATRIX_DECAY)
    glu_came, in_res, out_res, down_res = together(glu_came, in_res, out_res, down_res)
    glu_grad = join_columns(glu_came, 2, line_order, LINE).astype(f32)
    glu_res = adam_step(glu_w, glu_m, glu_v, glu_grad, factor, MATRIX_RATE, MATRIX_DECAY)
    gain_res = adam_step(gains, gain_m, gain_v, gain_grad, factor, GAIN_RATE, 0.0)
    return (
        block_out,
        grad_block[None],
        in_res[2],
        out_res[2],
        glu_res[2],
        down_res[2],
        gain_res[2],
        in_res[0],
        out_res[0],
        glu_res[0],
        down_res[0],
        gain_res[0],
        in_res[1],
        out_res[1],
        glu_res[1],
        down_res[1],
        gain_res[1],
        grad_norm,
    )


def split_mesh(mesh):
    seq, cores = mesh.shape["seq"], mesh.shape["rep"]
    side = 1
    while (2 * side) ** 3 <= seq:
        side *= 2
    return Mesh(
        mesh.devices.reshape(seq // (side * side), side, side, cores), (LINE,) + PLANE + (CORE,)
    )


def solution(mesh):
    tokens = P(CORE, (LINE,) + PLANE, None)
    matrix = P((LINE,) + PLANE + (CORE,), None)
    vectors = P(None, (LINE,) + PLANE + (CORE,))
    state = (matrix, matrix, matrix, matrix, vectors)
    return jax.shard_map(
        on_device,
        mesh=split_mesh(mesh),
        in_specs=(tokens, tokens, P(), P(), P((LINE,) + PLANE)) + state * 3,
        out_specs=(tokens, tokens) + state * 3 + (P(),),
        check_vma=False,
    )
```

```python
import functools

import jax
import jax.numpy as jnp
import numpy as np
from jax import lax
from jax.experimental import pallas as pl
from jax.experimental.pallas import tpu as pltpu
from jax.sharding import Mesh, PartitionSpec as P

STEP = 10

NORM_EPS = 1e-06
CLIP_LIMIT = 1.0
BETA_FIRST = 0.9
BETA_SECOND = 0.95
ADAM_EPS = 1e-08
MATRIX_RATE = 0.04
GAIN_RATE = 0.4
MATRIX_DECAY = 0.1

LINE = "z"
PLANE = ("y", "x")
CORE = "core"
MIXER_OWNERS = ("z", "core")
GLU_OWNERS = ("y", "x", "core")


def contract(left_side, right_side, left_dim, right_dim):
    return lax.dot_general(
        left_side,
        right_side,
        (((left_dim,), (right_dim,)), ((), ())),
        preferred_element_type=jnp.float32,
    )


def rounded(values):
    return lax.reduce_precision(values, exponent_bits=8, mantissa_bits=7)


def silu_slope(values):
    logistic = jax.nn.sigmoid(values)
    return logistic * (1.0 + values * (1.0 - logistic))


def sequence_weights(domain_ids, domain_weight):
    kinds = domain_weight.shape[0]
    total = domain_ids.shape[0]
    same_kind = (domain_ids[:, None] == domain_ids[None, :]).astype(jnp.float32)
    counts = jnp.sum(same_kind, axis=1)
    onehot = (domain_ids[:, None] == jnp.arange(kinds, dtype=jnp.int32)[None, :]).astype(
        jnp.float32
    )
    chosen = jnp.sum(onehot * domain_weight[None, :], axis=1)
    return chosen * (total / kinds) / counts


def adam_step(weight, first, second_m, grad, factor, rate, decay):
    clipped = grad * factor
    first_new = BETA_FIRST * first + (1.0 - BETA_FIRST) * clipped
    second_new = BETA_SECOND * second_m + (1.0 - BETA_SECOND) * clipped * clipped
    first_hat = first_new / (1.0 - BETA_FIRST**STEP)
    second_hat = second_new / (1.0 - BETA_SECOND**STEP)
    weight_new = weight - rate * (first_hat / (jnp.sqrt(second_hat) + ADAM_EPS) + decay * weight)
    return (first_new, second_new, weight_new)


def squared(values):
    values = values.astype(jnp.float32)
    return jnp.sum(values * values)


def swap(values, axis, bit):
    size = lax.axis_size(axis)
    return lax.ppermute(values, axis, [(i, i ^ bit) for i in range(size)])


def gather_small(values, axis):
    size = lax.axis_size(axis)
    held = lax.dynamic_update_index_in_dim(
        jnp.zeros((size,) + values.shape, values.dtype), values, lax.axis_index(axis), 0
    )
    bit = 1
    while bit < size:
        held = held + swap(held, axis, bit)
        bit *= 2
    return held


def total_small(values, groups):
    for axes in groups:
        terms = [values] + [swap(values, axes, k) for k in range(1, lax.axis_size(axes))]
        while len(terms) > 1:
            terms = [terms[i] + terms[i + 1] for i in range(0, len(terms), 2)]
        values = terms[0]
    return values


def gather_near(values, axes):
    size = lax.axis_size(axes)
    direct = [k for k in range(1, size) if axes != LINE or k & (k - 1) == 0]
    return {0: values} | {k: swap(values, axes, k) for k in direct}


def gather_far(blocks, axes):
    blocks = dict(blocks)
    for k in range(1, lax.axis_size(axes)):
        if k not in blocks:
            blocks[k] = swap(blocks[k ^ (k & -k)], axes, k & -k)
    return [blocks[k] for k in range(lax.axis_size(axes))]


def gather_tokens(values, axes):
    return jnp.concatenate(gather_far(gather_near(values, axes), axes), axis=0)


def scatter_far(partial, axes):
    size = lax.axis_size(axes)
    rows = partial.shape[0] // size
    blocks = {k: partial[k * rows : (k + 1) * rows] for k in range(size)}
    for k in range(size - 1, 0, -1):
        if axes == LINE and k & (k - 1):
            near = k & -k
            moved = swap(blocks.pop(k).astype(jnp.bfloat16), axes, near)
            blocks[k ^ near] = blocks[k ^ near] + moved.astype(jnp.float32)
    return blocks


def scatter_near(blocks, axes):
    total = blocks[0]
    for k in sorted(blocks, reverse=True)[:-1]:
        total = total + swap(blocks[k].astype(jnp.bfloat16), axes, k).astype(jnp.float32)
    return total


def scatter_tokens(partial, axes):
    return scatter_near(scatter_far(partial, axes), axes)


def total_tokens(values, axes):
    size = lax.axis_size(axes)
    blocks = values.reshape(size, values.shape[0] // size)
    bit = 1
    while bit < size:
        other = swap(blocks, axes, bit)
        blocks = blocks + jnp.stack([other[k ^ bit] for k in range(size)])
        bit *= 2
    return blocks.reshape(values.shape)


def core_sums(part, axes):
    size, cores = lax.axis_size(axes), lax.axis_size(CORE)
    core = lax.axis_index(CORE)
    blocks = part.reshape(size, cores, part.shape[0] // (size * cores), part.shape[1])
    total = lax.dynamic_index_in_dim(blocks, core, 1, keepdims=False).astype(jnp.float32)
    for k in range(1, cores):
        sent = lax.dynamic_index_in_dim(blocks, core ^ k, 1, keepdims=False)
        total = total + swap(sent, CORE, k).astype(jnp.float32)
    return total.astype(jnp.bfloat16)


def rank_sums(blocks, axes):
    rank = lax.axis_index(axes)
    total = lax.dynamic_index_in_dim(blocks, rank, 0, keepdims=False).astype(jnp.float32)
    for k in range(1, lax.axis_size(axes)):
        sent = lax.dynamic_index_in_dim(blocks, rank ^ k, 0, keepdims=False)
        total = total + swap(sent, axes, k).astype(jnp.float32)
    return total


def in_order(blocks, axes):
    rank = lax.axis_index(axes)
    blocks = jnp.stack(blocks)
    return jnp.concatenate(
        [lax.dynamic_index_in_dim(blocks, rank ^ k, 0) for k in range(blocks.shape[0])], axis=0
    )


def core_pair(values):
    return in_order([values] + [swap(values, CORE, k) for k in range(1, lax.axis_size(CORE))], CORE)


def send_each(blocks, axes):
    return [blocks[0]] + [swap(blocks[k], axes, k) for k in range(1, len(blocks))]


def rank_blocks(blocks, axes):
    rank = lax.axis_index(axes)
    return [
        lax.dynamic_index_in_dim(blocks, rank ^ k, 0, keepdims=False)
        for k in range(blocks.shape[0])
    ]


def together(*values):
    return lax.optimization_barrier(values)


def split_kernel(groups, order_ref, values_ref, out_ref):
    count, _, held = out_ref.shape
    unit = held // groups
    for k in range(count):
        for g in range(groups):
            start = pl.multiple_of((g * count + order_ref[k]) * unit, unit)
            out_ref[k, :, g * unit : (g + 1) * unit] = values_ref[:, pl.ds(start, unit)].astype(
                out_ref.dtype
            )


def split_columns(values, groups, order):
    count = order.shape[0]
    rows, width = values.shape
    unit = width // (groups * count)
    if unit % 128:
        blocks = values.astype(jnp.bfloat16).reshape(rows, groups, count, unit)
        blocks = blocks.transpose(2, 0, 1, 3).reshape(count, rows, groups * unit)
        return jnp.stack(
            [lax.dynamic_index_in_dim(blocks, order[k], 0, keepdims=False) for k in range(count)]
        )
    vmem = pl.BlockSpec(memory_space=pltpu.VMEM)
    return pl.pallas_call(
        functools.partial(split_kernel, groups),
        out_shape=jax.ShapeDtypeStruct((count, rows, groups * unit), jnp.bfloat16),
        in_specs=[pl.BlockSpec(memory_space=pltpu.SMEM), vmem],
        out_specs=vmem,
        compiler_params=pltpu.CompilerParams(vmem_limit_bytes=32 * 1024 * 1024),
    )(order, values)


def join_kernel(groups, order_ref, *refs):
    *came_refs, out_ref = refs
    count = len(came_refs)
    unit = out_ref.shape[1] // (groups * count)
    for k, came_ref in enumerate(came_refs):
        for g in range(groups):
            start = pl.multiple_of((g * count + order_ref[k]) * unit, unit)
            out_ref[:, pl.ds(start, unit)] = came_ref[:, g * unit : (g + 1) * unit]


def join_columns(came, groups, order, axes):
    rows, held = came[0].shape
    unit = held // groups
    if unit % 128:
        blocks = in_order(came, axes)
        return jnp.concatenate(
            [block[:, g * unit : (g + 1) * unit] for g in range(groups) for block in blocks], axis=1
        )
    vmem = pl.BlockSpec(memory_space=pltpu.VMEM)
    return pl.pallas_call(
        functools.partial(join_kernel, groups),
        out_shape=jax.ShapeDtypeStruct((rows, held * len(came)), came[0].dtype),
        in_specs=[pl.BlockSpec(memory_space=pltpu.SMEM)] + [vmem] * len(came),
        out_specs=vmem,
        compiler_params=pltpu.CompilerParams(vmem_limit_bytes=32 * 1024 * 1024),
    )(order, *came)


def turn_kernel(groups, outer, inner, values_ref, out_ref):
    unit = out_ref.shape[1] // (groups * outer * inner)
    for g in range(groups):
        for i in range(outer):
            for j in range(inner):
                old, new = (g * outer + i) * inner + j, (g * inner + j) * outer + i
                out_ref[:, new * unit : (new + 1) * unit] = values_ref[
                    :, old * unit : (old + 1) * unit
                ].astype(out_ref.dtype)


def turn_columns(values, groups, outer, inner, dtype):
    rows, width = values.shape
    unit = width // (groups * outer * inner)
    if unit % 64:
        values = values.astype(dtype).reshape(rows, groups, outer, inner, unit)
        return values.transpose(0, 1, 3, 2, 4).reshape(rows, width)
    vmem = pl.BlockSpec(memory_space=pltpu.VMEM)
    return pl.pallas_call(
        functools.partial(turn_kernel, groups, outer, inner),
        out_shape=jax.ShapeDtypeStruct((rows, width), dtype),
        in_specs=[vmem],
        out_specs=vmem,
        compiler_params=pltpu.CompilerParams(vmem_limit_bytes=32 * 1024 * 1024),
    )(values)


TILE = 8


def gates(proj_ref, rows, width, bound):
    in_raw = proj_ref[rows, 0:width].astype(jnp.bfloat16).astype(jnp.float32)
    forget_raw = proj_ref[rows, width : 2 * width].astype(jnp.bfloat16).astype(jnp.float32)
    forget = bound + (1.0 - bound) * jax.nn.sigmoid(forget_raw)
    return in_raw, forget


def scan_kernel(width, order_ref, proj_ref, bound_ref, state_ref, prod_ref, last_ref):
    blocks = order_ref.shape[0]
    per_block = proj_ref.shape[0] // blocks // TILE
    bound = bound_ref[0:1, :]
    row = lax.broadcasted_iota(jnp.int32, (TILE, width), 0)

    def step(index, carry):
        state_in, prod_in = carry
        tile = order_ref[index // per_block] * per_block + index % per_block
        rows = pl.ds(pl.multiple_of(tile * TILE, TILE), TILE)
        in_raw, forget = gates(proj_ref, rows, width, bound)
        drive = in_raw * jax.nn.sigmoid(in_raw) * (1.0 - forget)
        for shift in (1, 2, 4):
            keep = row >= shift
            drive = jnp.where(keep, forget * pltpu.roll(drive, shift, 0) + drive, drive)
            forget = jnp.where(keep, forget * pltpu.roll(forget, shift, 0), forget)
        state = drive + forget * state_in
        prod = forget * prod_in
        state_ref[rows, :] = state
        prod_ref[rows, :] = prod
        return state[TILE - 1 : TILE, :], prod[TILE - 1 : TILE, :]

    state, prod = lax.fori_loop(
        0,
        blocks * per_block,
        step,
        (jnp.zeros((1, width), jnp.float32), jnp.ones((1, width), jnp.float32)),
    )
    last_ref[0:1, :] = state
    last_ref[1:2, :] = prod


def back_kernel(width, order_ref, proj_ref, bound_ref, grad_ref, carried_ref, prod_ref, last_ref):
    blocks = order_ref.shape[0]
    per_block = proj_ref.shape[0] // blocks // TILE
    count = blocks * per_block
    bound = bound_ref[0:1, :]
    row = lax.broadcasted_iota(jnp.int32, (TILE, width), 0)

    def step(back, carry):
        carried_in, prod_in, forget_next = carry
        index = count - 1 - back
        tile = order_ref[index // per_block] * per_block + index % per_block
        rows = pl.ds(pl.multiple_of(tile * TILE, TILE), TILE)
        _, forget = gates(proj_ref, rows, width, bound)
        rate = jnp.where(row < TILE - 1, pltpu.roll(forget, TILE - 1, 0), forget_next)
        carried = grad_ref[rows, :].astype(jnp.float32)
        for shift in (1, 2, 4):
            keep = row < TILE - shift
            carried = jnp.where(
                keep, rate * pltpu.roll(carried, TILE - shift, 0) + carried, carried
            )
            rate = jnp.where(keep, rate * pltpu.roll(rate, TILE - shift, 0), rate)
        carried = carried + rate * carried_in
        prod = rate * prod_in
        carried_ref[rows, :] = carried
        prod_ref[rows, :] = prod
        return carried[0:1, :], prod[0:1, :], forget[0:1, :]

    ones = jnp.ones((1, width), jnp.float32)
    carried, prod, forget = lax.fori_loop(
        0, count, step, (jnp.zeros((1, width), jnp.float32), ones, ones)
    )
    last_ref[0:1, :] = forget * carried
    last_ref[1:2, :] = forget * prod


def call_scan(kernel, order, *arrays):
    tokens = arrays[0].shape[0]
    width = arrays[1].shape[1]
    vmem = pl.BlockSpec(memory_space=pltpu.VMEM)
    full = jax.ShapeDtypeStruct((tokens, width), jnp.float32)
    return pl.pallas_call(
        functools.partial(kernel, width),
        out_shape=(full, full, jax.ShapeDtypeStruct((2, width), jnp.float32)),
        in_specs=[pl.BlockSpec(memory_space=pltpu.SMEM)] + [vmem] * len(arrays),
        out_specs=(vmem, vmem, vmem),
        compiler_params=pltpu.CompilerParams(vmem_limit_bytes=32 * 1024 * 1024),
    )(order, *arrays)


def on_device(
    block_in,
    cotangent,
    domain_ids,
    domain_weight,
    lower_bound,
    in_w,
    out_w,
    glu_w,
    down_w,
    gains,
    in_m,
    out_m,
    glu_m,
    down_m,
    gain_m,
    in_v,
    out_v,
    glu_v,
    down_v,
    gain_v,
):
    bf16 = jnp.bfloat16
    f32 = jnp.float32
    inputs_f = block_in[0].astype(f32)
    tok, width = inputs_f.shape
    line = lax.axis_size(LINE)
    plane = lax.axis_size(PLANE)
    cores = lax.axis_size(CORE)
    level = lax.axis_index(LINE)
    rank = lax.axis_index(PLANE)
    device = lax.axis_index((LINE,) + PLANE)
    order = jnp.arange(plane, dtype=jnp.int32) ^ rank
    group_seqs = domain_ids.shape[0] // cores
    assert group_seqs == 1
    span = tok * line * plane
    rows = in_w.shape[0]
    chan = lower_bound.shape[0]
    channels = chan * line
    hidden_width = down_w.shape[0] * plane * cores

    seq_scale = sequence_weights(domain_ids, domain_weight)
    position = device * tok + jnp.arange(tok, dtype=jnp.int32)
    owner_seq = lax.axis_index(CORE) * group_seqs + position // (span // group_seqs)
    pick = (owner_seq[:, None] == jnp.arange(domain_ids.shape[0], dtype=jnp.int32)[None, :]).astype(
        f32
    )
    row_weight = jnp.sum(pick * seq_scale[None, :], axis=1)


    line_order = jnp.arange(line, dtype=jnp.int32) ^ level
    glu_came = send_each(split_columns(glu_w, 2, line_order), LINE)
    glu_held = in_order(glu_came, LINE).reshape(line * rows, 2 * hidden_width)
    in_came = send_each(split_columns(in_w, 3 * line, order), PLANE)
    in_held = in_order(in_came, PLANE).reshape(plane * rows, 3 * channels)

    gain_size = 3 * gains.shape[1]
    packed = jnp.concatenate([rounded(gains).reshape(-1), lower_bound])
    packed = gather_small(packed, LINE)
    bound = packed[:, gain_size:].reshape(1, channels)
    held_gains = gather_small(packed[:, :gain_size], CORE)
    gain_mid = (
        held_gains.reshape(cores, line, 3, gains.shape[1])[:, :, 1]
        .transpose(1, 0, 2)
        .reshape(1, channels)
    )
    held_gains = gather_small(gather_small(held_gains, "x"), "y")
    gain_f = (
        held_gains.reshape(plane, cores, line, 3, gains.shape[1])
        .transpose(3, 2, 0, 1, 4)
        .reshape(3, width)
    )

    in_held, glu_held = together(in_held, glu_held)
    in_b = lax.all_gather(in_held, MIXER_OWNERS, axis=0, tiled=True)

    scale_one = lax.rsqrt(jnp.mean(inputs_f * inputs_f, axis=1, keepdims=True) + NORM_EPS)
    unit_one = inputs_f * scale_one
    normed = turn_columns(unit_one * gain_f[0], line, plane, cores, bf16)
    normed = gather_tokens(normed, PLANE)
    normed, in_b, glu_held = together(normed, in_b, glu_held)
    proj = contract(normed, in_b, 1, 0)

    glu_b = lax.all_gather(glu_held, GLU_OWNERS, axis=0, tiled=True)
    out_pair = core_pair(out_w.astype(bf16))
    out_blocks = gather_near(out_pair, LINE)
    proj, out_blocks = together(proj, out_blocks)
    out_blocks = gather_far(out_blocks, LINE)
    local_state, local_prod, last = call_scan(scan_kernel, order, proj, bound)
    lasts = in_order([last] + [swap(last, LINE, k) for k in range(1, line)], LINE)
    lasts, out_blocks = together(lasts, out_blocks)
    state_in = jnp.zeros((channels,), f32)
    for k in range(line):
        state_in = jnp.where(k < level, lasts[k, 1] * state_in + lasts[k, 0], state_in)
    state = local_state + local_prod * state_in[None, :]
    state_f = rounded(state)
    square_mid = total_tokens(jnp.sum(state_f * state_f, axis=1), PLANE)
    out_b = in_order(out_blocks, LINE).reshape(channels, width)
    scale_mid = lax.rsqrt(square_mid / width + NORM_EPS)[:, None]
    unit_mid = state_f * scale_mid
    gate_raw = proj[:, 2 * channels :]
    gate_act = jax.nn.silu(gate_raw)
    gated = (unit_mid * gain_mid * gate_act).astype(bf16)
    grad_output = cotangent[0].astype(f32) * row_weight[:, None]
    gated, grad_output_b = together(gated, grad_output.astype(bf16))
    grad_output_b = gather_near(grad_output_b, LINE)
    mixed = scatter_tokens(contract(gated, out_b, 1, 0), PLANE)
    mixed, grad_output_b = together(mixed, grad_output_b)
    resid = inputs_f + mixed

    scale_two = lax.rsqrt(jnp.mean(resid * resid, axis=1, keepdims=True) + NORM_EPS)
    unit_two = resid * scale_two
    second_own = turn_columns(unit_two * gain_f[2], 1, line, plane * cores, bf16)
    second_own, down_own, glu_b = together(second_own, down_w.astype(bf16), glu_b)
    down_b = lax.all_gather(down_own, GLU_OWNERS, axis=0, tiled=True)
    second, glu_b = together(gather_near(second_own, LINE), glu_b)
    second = jnp.concatenate(gather_far(second, LINE), axis=0)
    second, grad_output_b = together(second, grad_output_b)
    paired = contract(second, glu_b, 1, 0)
    up_gate = paired[:, :hidden_width]
    up_value = paired[:, hidden_width:]
    gate_silu = jax.nn.silu(up_gate)
    hidden = (gate_silu * up_value).astype(bf16)

    grad_output_b = jnp.concatenate(gather_far(grad_output_b, LINE), axis=0)
    grad_hidden = contract(grad_output_b, down_b, 1, 1)
    grad_paired = jnp.concatenate(
        [grad_hidden * up_value * silu_slope(up_gate), grad_hidden * gate_silu], axis=1
    ).astype(bf16)
    second_part = contract(grad_paired, glu_b, 1, 1)
    grad_second = scatter_tokens(second_part, LINE)
    grad_second = turn_columns(grad_second, 1, plane * cores, line, f32)
    glu_part = contract(second, grad_paired, 0, 0).astype(bf16)
    glu_held = lax.psum_scatter(glu_part, GLU_OWNERS, scatter_dimension=0, tiled=True)
    down_part = contract(hidden, grad_output_b, 0, 0).astype(bf16)
    down_sums = core_sums(down_part, PLANE)
    grad_gain_two = jnp.sum(grad_second * unit_two, axis=0)
    weighted_two = grad_second * gain_f[2]
    grad_resid = grad_output + scale_two * (
        weighted_two - unit_two * jnp.mean(weighted_two * unit_two, axis=1, keepdims=True)
    )

    grad_resid, hidden = together(grad_resid, hidden)
    output = resid + scatter_tokens(contract(hidden, down_b, 1, 0), LINE)
    block_out = output.astype(bf16)[None]

    grad_resid_b = gather_tokens(grad_resid.astype(bf16), PLANE)
    grad_resid_b, block_out, down_sums = together(grad_resid_b, block_out, down_sums)
    grad_gated = contract(grad_resid_b, out_b, 1, 1)
    out_part = contract(gated, grad_resid_b, 0, 0).astype(bf16)
    grad_gain_mid = jnp.sum(grad_gated * unit_mid * gate_act, axis=0)
    grad_gate = grad_gated * unit_mid * gain_mid * silu_slope(gate_raw)
    weighted_mid = grad_gated * gain_mid * gate_act
    mean_mid = total_tokens(jnp.sum(weighted_mid * unit_mid, axis=1), PLANE) / width
    out_part, glu_held = together(out_part, glu_held)
    out_grad = lax.psum_scatter(out_part, MIXER_OWNERS, scatter_dimension=0, tiled=True)
    grad_state = scale_mid * (weighted_mid - unit_mid * mean_mid[:, None])
    local_carried, local_rate, first = call_scan(
        back_kernel, order, proj, bound, rounded(grad_state)
    )
    firsts = in_order([first] + [swap(first, LINE, k) for k in range(1, line)], LINE)
    carried_in = jnp.zeros((channels,), f32)
    for k in range(line - 1, -1, -1):
        carried_in = jnp.where(k > level, firsts[k, 1] * carried_in + firsts[k, 0], carried_in)
    carried = local_carried + local_rate * carried_in[None, :]
    blocked = state.reshape(plane, tok, channels)
    tails = lax.dynamic_update_index_in_dim(
        jnp.zeros((plane, channels), f32), state_in, order[0], 0
    )
    for k in range(1, plane):
        tails = lax.dynamic_update_index_in_dim(
            tails,
            lax.dynamic_index_in_dim(blocked, order[k - 1], 0, keepdims=False)[tok - 1],
            order[k],
            0,
        )
    previous = jnp.concatenate([tails[:, None], blocked[:, :-1]], axis=1).reshape(state.shape)
    in_raw = rounded(proj[:, :channels])
    forget_sig = jax.nn.sigmoid(rounded(proj[:, channels : 2 * channels]))
    forget = bound + (1.0 - bound) * forget_sig
    grad_in_raw = carried * (1.0 - forget) * silu_slope(in_raw)
    grad_forget_raw = (
        carried
        * (previous - jax.nn.silu(in_raw))
        * (1.0 - bound)
        * forget_sig
        * (1.0 - forget_sig)
    )
    grad_proj = jnp.concatenate([grad_in_raw, grad_forget_raw, grad_gate], axis=1).astype(bf16)
    in_part = contract(normed, grad_proj, 0, 0).astype(bf16)
    in_held = lax.psum_scatter(in_part, MIXER_OWNERS, scatter_dimension=0, tiled=True)
    down_grad = rank_sums(down_sums, PLANE)
    grad_normed = scatter_tokens(contract(grad_proj, in_b, 1, 1), PLANE)
    grad_normed = turn_columns(grad_normed, line, cores, plane, f32)
    grad_gain_one = jnp.sum(grad_normed * unit_one, axis=0)
    weighted_one = grad_normed * gain_f[0]
    grad_block = grad_resid + scale_one * (
        weighted_one - unit_one * jnp.mean(weighted_one * unit_one, axis=1, keepdims=True)
    )

    mid_row = lax.dynamic_update_index_in_dim(
        jnp.zeros((line, plane, chan), f32), grad_gain_mid.reshape(line, chan), rank, 1
    ).reshape(width)
    gain_part = jnp.stack([grad_gain_one, mid_row, grad_gain_two])
    early_squares = squared(glu_held) + squared(down_grad) + squared(out_grad)
    glu_sent = rank_blocks(glu_held.reshape(line, rows, 2 * hidden_width), LINE)
    in_held, glu_sent, gain_part, early_squares, grad_block = together(
        in_held, glu_sent, gain_part, early_squares, grad_block
    )
    glu_came = send_each(glu_sent, LINE)
    squares = jnp.broadcast_to(early_squares + squared(in_held), (1, width))
    totals = total_small(
        jnp.concatenate([gain_part, squares], axis=0), (LINE, PLANE, CORE)
    )
    in_blocks = in_held.reshape(plane, rows, 3 * channels)
    in_came = send_each(rank_blocks(in_blocks, PLANE), PLANE)
    gain_total = totals[:3]
    squares = totals[3, 0] + squared(gain_total)
    out_grad = out_grad.astype(f32)
    columns = gains.shape[1]
    gain_grad = lax.dynamic_slice_in_dim(
        gain_total, (device * cores + lax.axis_index(CORE)) * columns, columns, 1
    )
    grad_norm = jnp.sqrt(squares)
    factor = jnp.minimum(1.0, CLIP_LIMIT / (grad_norm + 1e-06))
    out_res = adam_step(out_w, out_m, out_v, out_grad, factor, MATRIX_RATE, MATRIX_DECAY)
    down_res = adam_step(down_w, down_m, down_v, down_grad, factor, MATRIX_RATE, MATRIX_DECAY)
    in_came, out_res, down_res = together(in_came, out_res, down_res)
    in_grad = join_columns(in_came, 3 * line, order, PLANE).astype(f32)
    in_res = adam_step(in_w, in_m, in_v, in_grad, factor, MATRIX_RATE, MATRIX_DECAY)
    glu_came, in_res = together(glu_came, in_res)
    glu_grad = join_columns(glu_came, 2, line_order, LINE).astype(f32)
    glu_res = adam_step(glu_w, glu_m, glu_v, glu_grad, factor, MATRIX_RATE, MATRIX_DECAY)
    gain_res = adam_step(gains, gain_m, gain_v, gain_grad, factor, GAIN_RATE, 0.0)
    return (
        block_out,
        grad_block[None],
        in_res[2],
        out_res[2],
        glu_res[2],
        down_res[2],
        gain_res[2],
        in_res[0],
        out_res[0],
        glu_res[0],
        down_res[0],
        gain_res[0],
        in_res[1],
        out_res[1],
        glu_res[1],
        down_res[1],
        gain_res[1],
        grad_norm,
    )


def split_mesh(mesh):
    seq, cores = mesh.shape["seq"], mesh.shape["rep"]
    side = 1
    while (2 * side) ** 3 <= seq:
        side *= 2
    return Mesh(
        mesh.devices.reshape(seq // (side * side), side, side, cores), (LINE,) + PLANE + (CORE,)
    )


def solution(mesh):
    tokens = P(CORE, (LINE,) + PLANE, None)
    matrix = P((LINE,) + PLANE + (CORE,), None)
    vectors = P(None, (LINE,) + PLANE + (CORE,))
    state = (matrix, matrix, matrix, matrix, vectors)
    return jax.shard_map(
        on_device,
        mesh=split_mesh(mesh),
        in_specs=(tokens, tokens, P(), P(), P((LINE,) + PLANE)) + state * 3,
        out_specs=(tokens, tokens) + state * 3 + (P(),),
        check_vma=False,
    )
```

```python
import functools

import jax
import jax.numpy as jnp
import numpy as np
from jax import lax
from jax.experimental import pallas as pl
from jax.experimental.pallas import tpu as pltpu
from jax.sharding import Mesh, PartitionSpec as P

STEP = 10

NORM_EPS = 1e-06
CLIP_LIMIT = 1.0
BETA_FIRST = 0.9
BETA_SECOND = 0.95
ADAM_EPS = 1e-08
MATRIX_RATE = 0.04
GAIN_RATE = 0.4
MATRIX_DECAY = 0.1

LINE = "z"
PLANE = ("y", "x")
CORE = "core"
MIXER_OWNERS = ("z", "core")
GLU_OWNERS = ("y", "x", "core")


def contract(left_side, right_side, left_dim, right_dim):
    return lax.dot_general(
        left_side,
        right_side,
        (((left_dim,), (right_dim,)), ((), ())),
        preferred_element_type=jnp.float32,
    )


def rounded(values):
    return lax.reduce_precision(values, exponent_bits=8, mantissa_bits=7)


def silu_slope(values):
    logistic = jax.nn.sigmoid(values)
    return logistic * (1.0 + values * (1.0 - logistic))


def sequence_weights(domain_ids, domain_weight):
    kinds = domain_weight.shape[0]
    total = domain_ids.shape[0]
    same_kind = (domain_ids[:, None] == domain_ids[None, :]).astype(jnp.float32)
    counts = jnp.sum(same_kind, axis=1)
    onehot = (domain_ids[:, None] == jnp.arange(kinds, dtype=jnp.int32)[None, :]).astype(
        jnp.float32
    )
    chosen = jnp.sum(onehot * domain_weight[None, :], axis=1)
    return chosen * (total / kinds) / counts


def adam_step(weight, first, second_m, grad, factor, rate, decay):
    clipped = grad * factor
    first_new = BETA_FIRST * first + (1.0 - BETA_FIRST) * clipped
    second_new = BETA_SECOND * second_m + (1.0 - BETA_SECOND) * clipped * clipped
    first_hat = first_new / (1.0 - BETA_FIRST**STEP)
    second_hat = second_new / (1.0 - BETA_SECOND**STEP)
    weight_new = weight - rate * (first_hat / (jnp.sqrt(second_hat) + ADAM_EPS) + decay * weight)
    return (first_new, second_new, weight_new)


def squared(values):
    values = values.astype(jnp.float32)
    return jnp.sum(values * values)


def swap(values, axis, bit):
    size = lax.axis_size(axis)
    return lax.ppermute(values, axis, [(i, i ^ bit) for i in range(size)])


def gather_small(values, axis):
    size = lax.axis_size(axis)
    held = lax.dynamic_update_index_in_dim(
        jnp.zeros((size,) + values.shape, values.dtype), values, lax.axis_index(axis), 0
    )
    bit = 1
    while bit < size:
        held = held + swap(held, axis, bit)
        bit *= 2
    return held


def total_small(values, groups):
    for axes in groups:
        terms = [values] + [swap(values, axes, k) for k in range(1, lax.axis_size(axes))]
        while len(terms) > 1:
            terms = [terms[i] + terms[i + 1] for i in range(0, len(terms), 2)]
        values = terms[0]
    return values


def gather_near(values, axes):
    size = lax.axis_size(axes)
    direct = [k for k in range(1, size) if axes != LINE or k & (k - 1) == 0]
    return {0: values} | {k: swap(values, axes, k) for k in direct}


def gather_far(blocks, axes):
    blocks = dict(blocks)
    for k in range(1, lax.axis_size(axes)):
        if k not in blocks:
            blocks[k] = swap(blocks[k ^ (k & -k)], axes, k & -k)
    return [blocks[k] for k in range(lax.axis_size(axes))]


def gather_tokens(values, axes):
    return jnp.concatenate(gather_far(gather_near(values, axes), axes), axis=0)


def scatter_far(partial, axes):
    size = lax.axis_size(axes)
    rows = partial.shape[0] // size
    blocks = {k: partial[k * rows : (k + 1) * rows] for k in range(size)}
    for k in range(size - 1, 0, -1):
        if axes == LINE and k & (k - 1):
            near = k & -k
            moved = swap(blocks.pop(k).astype(jnp.bfloat16), axes, near)
            blocks[k ^ near] = blocks[k ^ near] + moved.astype(jnp.float32)
    return blocks


def scatter_near(blocks, axes):
    total = blocks[0]
    for k in sorted(blocks, reverse=True)[:-1]:
        total = total + swap(blocks[k].astype(jnp.bfloat16), axes, k).astype(jnp.float32)
    return total


def scatter_tokens(partial, axes):
    return scatter_near(scatter_far(partial, axes), axes)


def total_tokens(values, axes):
    size = lax.axis_size(axes)
    blocks = values.reshape(size, values.shape[0] // size)
    bit = 1
    while bit < size:
        other = swap(blocks, axes, bit)
        blocks = blocks + jnp.stack([other[k ^ bit] for k in range(size)])
        bit *= 2
    return blocks.reshape(values.shape)


def core_sums(part, axes):
    size, cores = lax.axis_size(axes), lax.axis_size(CORE)
    core = lax.axis_index(CORE)
    blocks = part.reshape(size, cores, part.shape[0] // (size * cores), part.shape[1])
    total = lax.dynamic_index_in_dim(blocks, core, 1, keepdims=False).astype(jnp.float32)
    for k in range(1, cores):
        sent = lax.dynamic_index_in_dim(blocks, core ^ k, 1, keepdims=False)
        total = total + swap(sent, CORE, k).astype(jnp.float32)
    return total.astype(jnp.bfloat16)


def rank_sums(blocks, axes):
    rank = lax.axis_index(axes)
    total = lax.dynamic_index_in_dim(blocks, rank, 0, keepdims=False).astype(jnp.float32)
    for k in range(1, lax.axis_size(axes)):
        sent = lax.dynamic_index_in_dim(blocks, rank ^ k, 0, keepdims=False)
        total = total + swap(sent, axes, k).astype(jnp.float32)
    return total


def in_order(blocks, axes):
    rank = lax.axis_index(axes)
    blocks = jnp.stack(blocks)
    return jnp.concatenate(
        [lax.dynamic_index_in_dim(blocks, rank ^ k, 0) for k in range(blocks.shape[0])], axis=0
    )


def gather_pairs(blocks, axes):
    blocks = jnp.stack(blocks)
    cores = [blocks] + [swap(blocks, CORE, k) for k in range(1, lax.axis_size(CORE))]
    cores = in_order(cores, CORE).swapaxes(0, 1)
    return in_order(list(cores), axes).reshape(-1, blocks.shape[2])


def send_each(blocks, axes):
    return [blocks[0]] + [swap(blocks[k], axes, k) for k in range(1, len(blocks))]


def rank_blocks(blocks, axes):
    rank = lax.axis_index(axes)
    return [
        lax.dynamic_index_in_dim(blocks, rank ^ k, 0, keepdims=False)
        for k in range(blocks.shape[0])
    ]


def together(*values):
    return lax.optimization_barrier(values)


def split_kernel(groups, order_ref, values_ref, out_ref):
    count, _, held = out_ref.shape
    unit = held // groups
    for k in range(count):
        for g in range(groups):
            start = pl.multiple_of((g * count + order_ref[k]) * unit, unit)
            out_ref[k, :, g * unit : (g + 1) * unit] = values_ref[:, pl.ds(start, unit)].astype(
                out_ref.dtype
            )


def split_columns(values, groups, order):
    count = order.shape[0]
    rows, width = values.shape
    unit = width // (groups * count)
    if unit % 128:
        blocks = values.astype(jnp.bfloat16).reshape(rows, groups, count, unit)
        blocks = blocks.transpose(2, 0, 1, 3).reshape(count, rows, groups * unit)
        return jnp.stack(
            [lax.dynamic_index_in_dim(blocks, order[k], 0, keepdims=False) for k in range(count)]
        )
    vmem = pl.BlockSpec(memory_space=pltpu.VMEM)
    return pl.pallas_call(
        functools.partial(split_kernel, groups),
        out_shape=jax.ShapeDtypeStruct((count, rows, groups * unit), jnp.bfloat16),
        in_specs=[pl.BlockSpec(memory_space=pltpu.SMEM), vmem],
        out_specs=vmem,
        compiler_params=pltpu.CompilerParams(vmem_limit_bytes=32 * 1024 * 1024),
    )(order, values)


def join_kernel(groups, order_ref, *refs):
    *came_refs, out_ref = refs
    count = len(came_refs)
    unit = out_ref.shape[1] // (groups * count)
    for k, came_ref in enumerate(came_refs):
        for g in range(groups):
            start = pl.multiple_of((g * count + order_ref[k]) * unit, unit)
            out_ref[:, pl.ds(start, unit)] = came_ref[:, g * unit : (g + 1) * unit]


def join_columns(came, groups, order, axes):
    rows, held = came[0].shape
    unit = held // groups
    if unit % 128:
        blocks = in_order(came, axes)
        return jnp.concatenate(
            [block[:, g * unit : (g + 1) * unit] for g in range(groups) for block in blocks], axis=1
        )
    vmem = pl.BlockSpec(memory_space=pltpu.VMEM)
    return pl.pallas_call(
        functools.partial(join_kernel, groups),
        out_shape=jax.ShapeDtypeStruct((rows, held * len(came)), came[0].dtype),
        in_specs=[pl.BlockSpec(memory_space=pltpu.SMEM)] + [vmem] * len(came),
        out_specs=vmem,
        compiler_params=pltpu.CompilerParams(vmem_limit_bytes=32 * 1024 * 1024),
    )(order, *came)


def turn_kernel(groups, outer, inner, values_ref, out_ref):
    unit = out_ref.shape[1] // (groups * outer * inner)
    for g in range(groups):
        for i in range(outer):
            for j in range(inner):
                old, new = (g * outer + i) * inner + j, (g * inner + j) * outer + i
                out_ref[:, new * unit : (new + 1) * unit] = values_ref[
                    :, old * unit : (old + 1) * unit
                ].astype(out_ref.dtype)


def turn_columns(values, groups, outer, inner, dtype):
    rows, width = values.shape
    unit = width // (groups * outer * inner)
    if unit % 64:
        values = values.astype(dtype).reshape(rows, groups, outer, inner, unit)
        return values.transpose(0, 1, 3, 2, 4).reshape(rows, width)
    vmem = pl.BlockSpec(memory_space=pltpu.VMEM)
    return pl.pallas_call(
        functools.partial(turn_kernel, groups, outer, inner),
        out_shape=jax.ShapeDtypeStruct((rows, width), dtype),
        in_specs=[vmem],
        out_specs=vmem,
        compiler_params=pltpu.CompilerParams(vmem_limit_bytes=32 * 1024 * 1024),
    )(values)


TILE = 8


def gates(proj_ref, rows, width, bound):
    in_raw = proj_ref[rows, 0:width].astype(jnp.bfloat16).astype(jnp.float32)
    forget_raw = proj_ref[rows, width : 2 * width].astype(jnp.bfloat16).astype(jnp.float32)
    forget = bound + (1.0 - bound) * jax.nn.sigmoid(forget_raw)
    return in_raw, forget


def scan_kernel(width, order_ref, proj_ref, bound_ref, state_ref, prod_ref, last_ref):
    blocks = order_ref.shape[0]
    per_block = proj_ref.shape[0] // blocks // TILE
    bound = bound_ref[0:1, :]
    row = lax.broadcasted_iota(jnp.int32, (TILE, width), 0)

    def step(index, carry):
        state_in, prod_in = carry
        tile = order_ref[index // per_block] * per_block + index % per_block
        rows = pl.ds(pl.multiple_of(tile * TILE, TILE), TILE)
        in_raw, forget = gates(proj_ref, rows, width, bound)
        drive = in_raw * jax.nn.sigmoid(in_raw) * (1.0 - forget)
        for shift in (1, 2, 4):
            keep = row >= shift
            drive = jnp.where(keep, forget * pltpu.roll(drive, shift, 0) + drive, drive)
            forget = jnp.where(keep, forget * pltpu.roll(forget, shift, 0), forget)
        state = drive + forget * state_in
        prod = forget * prod_in
        state_ref[rows, :] = state
        prod_ref[rows, :] = prod
        return state[TILE - 1 : TILE, :], prod[TILE - 1 : TILE, :]

    state, prod = lax.fori_loop(
        0,
        blocks * per_block,
        step,
        (jnp.zeros((1, width), jnp.float32), jnp.ones((1, width), jnp.float32)),
    )
    last_ref[0:1, :] = state
    last_ref[1:2, :] = prod


def back_kernel(width, order_ref, proj_ref, bound_ref, grad_ref, carried_ref, prod_ref, last_ref):
    blocks = order_ref.shape[0]
    per_block = proj_ref.shape[0] // blocks // TILE
    count = blocks * per_block
    bound = bound_ref[0:1, :]
    row = lax.broadcasted_iota(jnp.int32, (TILE, width), 0)

    def step(back, carry):
        carried_in, prod_in, forget_next = carry
        index = count - 1 - back
        tile = order_ref[index // per_block] * per_block + index % per_block
        rows = pl.ds(pl.multiple_of(tile * TILE, TILE), TILE)
        _, forget = gates(proj_ref, rows, width, bound)
        rate = jnp.where(row < TILE - 1, pltpu.roll(forget, TILE - 1, 0), forget_next)
        carried = grad_ref[rows, :].astype(jnp.float32)
        for shift in (1, 2, 4):
            keep = row < TILE - shift
            carried = jnp.where(
                keep, rate * pltpu.roll(carried, TILE - shift, 0) + carried, carried
            )
            rate = jnp.where(keep, rate * pltpu.roll(rate, TILE - shift, 0), rate)
        carried = carried + rate * carried_in
        prod = rate * prod_in
        carried_ref[rows, :] = carried
        prod_ref[rows, :] = prod
        return carried[0:1, :], prod[0:1, :], forget[0:1, :]

    ones = jnp.ones((1, width), jnp.float32)
    carried, prod, forget = lax.fori_loop(
        0, count, step, (jnp.zeros((1, width), jnp.float32), ones, ones)
    )
    last_ref[0:1, :] = forget * carried
    last_ref[1:2, :] = forget * prod


def call_scan(kernel, order, *arrays):
    tokens = arrays[0].shape[0]
    width = arrays[1].shape[1]
    vmem = pl.BlockSpec(memory_space=pltpu.VMEM)
    full = jax.ShapeDtypeStruct((tokens, width), jnp.float32)
    return pl.pallas_call(
        functools.partial(kernel, width),
        out_shape=(full, full, jax.ShapeDtypeStruct((2, width), jnp.float32)),
        in_specs=[pl.BlockSpec(memory_space=pltpu.SMEM)] + [vmem] * len(arrays),
        out_specs=(vmem, vmem, vmem),
        compiler_params=pltpu.CompilerParams(vmem_limit_bytes=32 * 1024 * 1024),
    )(order, *arrays)


def on_device(
    block_in,
    cotangent,
    domain_ids,
    domain_weight,
    lower_bound,
    in_w,
    out_w,
    glu_w,
    down_w,
    gains,
    in_m,
    out_m,
    glu_m,
    down_m,
    gain_m,
    in_v,
    out_v,
    glu_v,
    down_v,
    gain_v,
):
    bf16 = jnp.bfloat16
    f32 = jnp.float32
    inputs_f = block_in[0].astype(f32)
    tok, width = inputs_f.shape
    line = lax.axis_size(LINE)
    plane = lax.axis_size(PLANE)
    cores = lax.axis_size(CORE)
    level = lax.axis_index(LINE)
    rank = lax.axis_index(PLANE)
    device = lax.axis_index((LINE,) + PLANE)
    order = jnp.arange(plane, dtype=jnp.int32) ^ rank
    group_seqs = domain_ids.shape[0] // cores
    assert group_seqs == 1
    span = tok * line * plane
    rows = in_w.shape[0]
    chan = lower_bound.shape[0]
    channels = chan * line
    hidden_width = down_w.shape[0] * plane * cores

    seq_scale = sequence_weights(domain_ids, domain_weight)
    position = device * tok + jnp.arange(tok, dtype=jnp.int32)
    owner_seq = lax.axis_index(CORE) * group_seqs + position // (span // group_seqs)
    pick = (owner_seq[:, None] == jnp.arange(domain_ids.shape[0], dtype=jnp.int32)[None, :]).astype(
        f32
    )
    row_weight = jnp.sum(pick * seq_scale[None, :], axis=1)


    line_order = jnp.arange(line, dtype=jnp.int32) ^ level
    glu_came = send_each(split_columns(glu_w, 2, line_order), LINE)
    glu_held = in_order(glu_came, LINE).reshape(line * rows, 2 * hidden_width)
    in_came = send_each(split_columns(in_w, 3 * line, order), PLANE)
    in_held = in_order(in_came, PLANE).reshape(plane * rows, 3 * channels)

    gain_size = 3 * gains.shape[1]
    packed = jnp.concatenate([rounded(gains).reshape(-1), lower_bound])
    packed = gather_small(packed, LINE)
    bound = packed[:, gain_size:].reshape(1, channels)
    held_gains = gather_small(packed[:, :gain_size], CORE)
    gain_mid = (
        held_gains.reshape(cores, line, 3, gains.shape[1])[:, :, 1]
        .transpose(1, 0, 2)
        .reshape(1, channels)
    )
    held_gains = gather_small(gather_small(held_gains, "x"), "y")
    gain_f = (
        held_gains.reshape(plane, cores, line, 3, gains.shape[1])
        .transpose(3, 2, 0, 1, 4)
        .reshape(3, width)
    )

    in_held, glu_held = together(in_held, glu_held)
    in_b = lax.all_gather(in_held, MIXER_OWNERS, axis=0, tiled=True)

    scale_one = lax.rsqrt(jnp.mean(inputs_f * inputs_f, axis=1, keepdims=True) + NORM_EPS)
    unit_one = inputs_f * scale_one
    normed = turn_columns(unit_one * gain_f[0], line, plane, cores, bf16)
    normed = gather_tokens(normed, PLANE)
    normed, out_own = together(normed, out_w.astype(bf16))
    out_blocks = gather_near(out_own, LINE)
    normed, in_b, glu_held = together(normed, in_b, glu_held)
    proj = contract(normed, in_b, 1, 0)

    glu_b = lax.all_gather(glu_held, GLU_OWNERS, axis=0, tiled=True)
    proj, out_blocks = together(proj, out_blocks)
    out_b = gather_pairs(gather_far(out_blocks, LINE), LINE)
    local_state, local_prod, last = call_scan(scan_kernel, order, proj, bound)
    lasts = in_order([last] + [swap(last, LINE, k) for k in range(1, line)], LINE)
    lasts, out_b = together(lasts, out_b)
    state_in = jnp.zeros((channels,), f32)
    for k in range(line):
        state_in = jnp.where(k < level, lasts[k, 1] * state_in + lasts[k, 0], state_in)
    state = local_state + local_prod * state_in[None, :]
    state_f = rounded(state)
    square_mid = total_tokens(jnp.sum(state_f * state_f, axis=1), PLANE)
    scale_mid = lax.rsqrt(square_mid / width + NORM_EPS)[:, None]
    unit_mid = state_f * scale_mid
    gate_raw = proj[:, 2 * channels :]
    gate_act = jax.nn.silu(gate_raw)
    gated = (unit_mid * gain_mid * gate_act).astype(bf16)
    grad_output = cotangent[0].astype(f32) * row_weight[:, None]
    gated, grad_output_b = together(gated, grad_output.astype(bf16))
    grad_output_b = gather_near(grad_output_b, LINE)
    mixed = scatter_tokens(contract(gated, out_b, 1, 0), PLANE)
    mixed, grad_output_b = together(mixed, grad_output_b)
    resid = inputs_f + mixed

    scale_two = lax.rsqrt(jnp.mean(resid * resid, axis=1, keepdims=True) + NORM_EPS)
    unit_two = resid * scale_two
    second_own = turn_columns(unit_two * gain_f[2], 1, line, plane * cores, bf16)
    second_own, down_own, glu_b = together(second_own, down_w.astype(bf16), glu_b)
    down_b = lax.all_gather(down_own, GLU_OWNERS, axis=0, tiled=True)
    second, glu_b = together(gather_near(second_own, LINE), glu_b)
    second = jnp.concatenate(gather_far(second, LINE), axis=0)
    second, grad_output_b = together(second, grad_output_b)
    paired = contract(second, glu_b, 1, 0)
    up_gate = paired[:, :hidden_width]
    up_value = paired[:, hidden_width:]
    gate_silu = jax.nn.silu(up_gate)
    hidden = (gate_silu * up_value).astype(bf16)

    grad_output_b = jnp.concatenate(gather_far(grad_output_b, LINE), axis=0)
    grad_hidden = contract(grad_output_b, down_b, 1, 1)
    grad_paired = jnp.concatenate(
        [grad_hidden * up_value * silu_slope(up_gate), grad_hidden * gate_silu], axis=1
    ).astype(bf16)
    second_part = contract(grad_paired, glu_b, 1, 1)
    grad_second = scatter_tokens(second_part, LINE)
    grad_second = turn_columns(grad_second, 1, plane * cores, line, f32)
    glu_part = contract(second, grad_paired, 0, 0).astype(bf16)
    glu_held = lax.psum_scatter(glu_part, GLU_OWNERS, scatter_dimension=0, tiled=True)
    down_part = contract(hidden, grad_output_b, 0, 0).astype(bf16)
    down_sums = core_sums(down_part, PLANE)
    grad_gain_two = jnp.sum(grad_second * unit_two, axis=0)
    weighted_two = grad_second * gain_f[2]
    grad_resid = grad_output + scale_two * (
        weighted_two - unit_two * jnp.mean(weighted_two * unit_two, axis=1, keepdims=True)
    )

    grad_resid, hidden = together(grad_resid, hidden)
    output = resid + scatter_tokens(contract(hidden, down_b, 1, 0), LINE)
    block_out = output.astype(bf16)[None]

    grad_resid_b = gather_tokens(grad_resid.astype(bf16), PLANE)
    grad_resid_b, block_out, down_sums = together(grad_resid_b, block_out, down_sums)
    grad_gated = contract(grad_resid_b, out_b, 1, 1)
    out_part = contract(gated, grad_resid_b, 0, 0).astype(bf16)
    grad_gain_mid = jnp.sum(grad_gated * unit_mid * gate_act, axis=0)
    grad_gate = grad_gated * unit_mid * gain_mid * silu_slope(gate_raw)
    weighted_mid = grad_gated * gain_mid * gate_act
    mean_mid = total_tokens(jnp.sum(weighted_mid * unit_mid, axis=1), PLANE) / width
    out_part, glu_held = together(out_part, glu_held)
    out_grad = lax.psum_scatter(out_part, MIXER_OWNERS, scatter_dimension=0, tiled=True)
    grad_state = scale_mid * (weighted_mid - unit_mid * mean_mid[:, None])
    local_carried, local_rate, first = call_scan(
        back_kernel, order, proj, bound, rounded(grad_state)
    )
    firsts = in_order([first] + [swap(first, LINE, k) for k in range(1, line)], LINE)
    carried_in = jnp.zeros((channels,), f32)
    for k in range(line - 1, -1, -1):
        carried_in = jnp.where(k > level, firsts[k, 1] * carried_in + firsts[k, 0], carried_in)
    carried = local_carried + local_rate * carried_in[None, :]
    blocked = state.reshape(plane, tok, channels)
    tails = lax.dynamic_update_index_in_dim(
        jnp.zeros((plane, channels), f32), state_in, order[0], 0
    )
    for k in range(1, plane):
        tails = lax.dynamic_update_index_in_dim(
            tails,
            lax.dynamic_index_in_dim(blocked, order[k - 1], 0, keepdims=False)[tok - 1],
            order[k],
            0,
        )
    previous = jnp.concatenate([tails[:, None], blocked[:, :-1]], axis=1).reshape(state.shape)
    in_raw = rounded(proj[:, :channels])
    forget_sig = jax.nn.sigmoid(rounded(proj[:, channels : 2 * channels]))
    forget = bound + (1.0 - bound) * forget_sig
    grad_in_raw = carried * (1.0 - forget) * silu_slope(in_raw)
    grad_forget_raw = (
        carried
        * (previous - jax.nn.silu(in_raw))
        * (1.0 - bound)
        * forget_sig
        * (1.0 - forget_sig)
    )
    grad_proj = jnp.concatenate([grad_in_raw, grad_forget_raw, grad_gate], axis=1).astype(bf16)
    in_part = contract(normed, grad_proj, 0, 0).astype(bf16)
    in_held = lax.psum_scatter(in_part, MIXER_OWNERS, scatter_dimension=0, tiled=True)
    down_grad = rank_sums(down_sums, PLANE)
    grad_normed = scatter_tokens(contract(grad_proj, in_b, 1, 1), PLANE)
    grad_normed = turn_columns(grad_normed, line, cores, plane, f32)
    grad_gain_one = jnp.sum(grad_normed * unit_one, axis=0)
    weighted_one = grad_normed * gain_f[0]
    grad_block = grad_resid + scale_one * (
        weighted_one - unit_one * jnp.mean(weighted_one * unit_one, axis=1, keepdims=True)
    )

    mid_row = lax.dynamic_update_index_in_dim(
        jnp.zeros((line, plane, chan), f32), grad_gain_mid.reshape(line, chan), rank, 1
    ).reshape(width)
    gain_part = jnp.stack([grad_gain_one, mid_row, grad_gain_two])
    early_squares = squared(glu_held) + squared(down_grad) + squared(out_grad)
    glu_sent = rank_blocks(glu_held.reshape(line, rows, 2 * hidden_width), LINE)
    in_held, glu_sent, gain_part, early_squares, grad_block = together(
        in_held, glu_sent, gain_part, early_squares, grad_block
    )
    glu_came = send_each(glu_sent, LINE)
    squares = jnp.broadcast_to(early_squares + squared(in_held), (1, width))
    totals = total_small(
        jnp.concatenate([gain_part, squares], axis=0), (LINE, PLANE, CORE)
    )
    in_blocks = in_held.reshape(plane, rows, 3 * channels)
    in_came = send_each(rank_blocks(in_blocks, PLANE), PLANE)
    gain_total = totals[:3]
    squares = totals[3, 0] + squared(gain_total)
    out_grad = out_grad.astype(f32)
    columns = gains.shape[1]
    gain_grad = lax.dynamic_slice_in_dim(
        gain_total, (device * cores + lax.axis_index(CORE)) * columns, columns, 1
    )
    grad_norm = jnp.sqrt(squares)
    factor = jnp.minimum(1.0, CLIP_LIMIT / (grad_norm + 1e-06))
    out_res = adam_step(out_w, out_m, out_v, out_grad, factor, MATRIX_RATE, MATRIX_DECAY)
    down_res = adam_step(down_w, down_m, down_v, down_grad, factor, MATRIX_RATE, MATRIX_DECAY)
    in_came, out_res, down_res = together(in_came, out_res, down_res)
    in_grad = join_columns(in_came, 3 * line, order, PLANE).astype(f32)
    in_res = adam_step(in_w, in_m, in_v, in_grad, factor, MATRIX_RATE, MATRIX_DECAY)
    glu_came, in_res = together(glu_came, in_res)
    glu_grad = join_columns(glu_came, 2, line_order, LINE).astype(f32)
    glu_res = adam_step(glu_w, glu_m, glu_v, glu_grad, factor, MATRIX_RATE, MATRIX_DECAY)
    gain_res = adam_step(gains, gain_m, gain_v, gain_grad, factor, GAIN_RATE, 0.0)
    return (
        block_out,
        grad_block[None],
        in_res[2],
        out_res[2],
        glu_res[2],
        down_res[2],
        gain_res[2],
        in_res[0],
        out_res[0],
        glu_res[0],
        down_res[0],
        gain_res[0],
        in_res[1],
        out_res[1],
        glu_res[1],
        down_res[1],
        gain_res[1],
        grad_norm,
    )


def split_mesh(mesh):
    seq, cores = mesh.shape["seq"], mesh.shape["rep"]
    side = 1
    while (2 * side) ** 3 <= seq:
        side *= 2
    return Mesh(
        mesh.devices.reshape(seq // (side * side), side, side, cores), (LINE,) + PLANE + (CORE,)
    )


def solution(mesh):
    tokens = P(CORE, (LINE,) + PLANE, None)
    matrix = P((LINE,) + PLANE + (CORE,), None)
    vectors = P(None, (LINE,) + PLANE + (CORE,))
    state = (matrix, matrix, matrix, matrix, vectors)
    return jax.shard_map(
        on_device,
        mesh=split_mesh(mesh),
        in_specs=(tokens, tokens, P(), P(), P((LINE,) + PLANE)) + state * 3,
        out_specs=(tokens, tokens) + state * 3 + (P(),),
        check_vma=False,
    )
```
